32 devices in a mesh: blk: 32 (over z, y, x, core).
Axes of the slice: x: 2, y: 2, z: 4, core: 2. Of those that a mesh axis runs over, the one named last changes fastest.
Arguments:
- diag_block: float32 [32, 512, 512], P('blk'), may hold values from -0.6 to 12.6, as said below
- near_blocks: float32 [32, 6, 512, 512], P('blk'), may hold values from -0.15 to 0.15
- far_coupling: float32 [32, 5, 256, 256], P('blk'), may hold values from -0.15 to 0.15
- leaf_basis: float32 [32, 512, 512], P('blk'), may hold values from -0.2 to 1.2
- parent_basis: float32 [8192, 1024], P('blk'), may hold values from -0.2 to 1.2
- near_index: int32 [32, 6], P('blk'), may hold values from 0 to 31, as said below
- far_index: int32 [32, 5], P('blk'), may hold values from 0 to 31, as said below
Outputs:
- leaf_factor: float32 [8192, 512], P('blk')
- parent_cholesky_factor: float32 [8192, 768], P('blk')
- parent_coupling: float32 [8192, 768], P('blk')
The draws below stay inside these ranges and needn't reach their ends.
Inputs may be any that keep to these rules, and one draw needn't show every extreme that they name: `near_index`: row i lists 6 different leaves, none equal to i, among the 12 leaves of parents i // 4 - 1, i // 4, i // 4 + 1 (modulo 8). `far_index`: row i lists the remaining 5 leaves of those parents: i, its near list and its far list name each of the 12 leaves once. `diag_block`: each block is symmetric.
All inputs are finite; a program needn't handle non-finite values.
Results may differ from the reference program's by a relative error of at most 0.0003.
Values sent between devices are 32-bit elements; how exact they have to be, the bound alone decides.
No kernel may reach another device: no remote copies, remote signals or barrier semaphores. Data moves between devices by JAX's collectives and lax.ppermute only.
A program may use at most 192 MiB of HBM per device.

```python
import jax
import jax.numpy as jnp
from jax import lax

LEAF = 512
RANK = 256
NEAR = 6
GROUP = 4
BLOCKS = 32
PARENTS = 8
REDUN = 256
PAR = 1024
PRED = 768
FAR = 5


def draw_diag_block(key, part):
    random_portion = jax.random.uniform(key, (BLOCKS, LEAF, LEAF), jnp.float32, -0.3, 0.3)
    symmetric = 0.5 * (random_portion + jnp.swapaxes(random_portion, 1, 2))
    identity = jnp.eye(LEAF, dtype=jnp.float32)
    return symmetric + 12.0 * identity[None]


def basis_noise(key, shape, order):
    spread = 0.2 / order ** 0.5
    return jnp.clip(jax.random.normal(key, shape, jnp.float32) * spread, -4.0 * spread, 4.0 * spread)


def draw_leaf_basis(key, part):
    identity = jnp.eye(LEAF, dtype=jnp.float32)
    return identity[None] + basis_noise(key, (BLOCKS, LEAF, LEAF), LEAF)


def draw_parent_basis(key, part):
    identity = jnp.tile(jnp.eye(PAR, dtype=jnp.float32), (PARENTS, 1))
    return identity + basis_noise(key, (PARENTS * PAR, PAR), PAR)


def window_lists(key):
    row_keys = jax.random.split(jax.random.fold_in(key, 7), BLOCKS)
    shuffled = jax.vmap(lambda row_key: jax.random.permutation(row_key, 3 * GROUP - 1))(row_keys).astype(jnp.int32)
    leaf_ids = jnp.arange(BLOCKS, dtype=jnp.int32)[:, None]
    own_column = GROUP + leaf_ids % GROUP
    columns = shuffled + (shuffled >= own_column).astype(jnp.int32)
    parent = leaf_ids // GROUP
    return ((GROUP * (parent - 1) + columns) % BLOCKS).astype(jnp.int32)


def draw_near_index(key, part):
    return window_lists(key)[:, :NEAR]


def draw_far_index(key, part):
    return window_lists(key)[:, NEAR:]


def levels(key, shape, cuts, smallest, high):
    gain, own = 1.0, jax.random.fold_in(key, 6)
    for axis_at, blocks in cuts:
        draws = jnp.exp(jax.random.uniform(jax.random.fold_in(own, axis_at), (blocks,), jnp.float32, smallest / len(cuts), high / len(cuts)))
        gain = gain * jnp.repeat(draws, shape[axis_at] // blocks).reshape([-1 if axis == axis_at else 1 for axis in range(len(shape))])
    return gain


def noise(stream_key, dims, deviation, bound, shards=(), held_as=jnp.bfloat16):
    gain = levels(stream_key, dims, shards, -0.22, 0.18) if shards else 1.0
    drawn = jax.random.normal(stream_key, dims, jnp.float32) * deviation * gain
    return jnp.minimum(jnp.maximum(drawn, -bound), bound).astype(held_as)


def setup_inputs(seed: int = 0) -> dict:
    keys = jax.random.split(jax.random.key(seed), 8)
    diag_block = draw_diag_block(jax.random.fold_in(keys[7], 71), 0)
    near_blocks = noise(keys[1], (BLOCKS, NEAR, LEAF, LEAF), 0.025, 0.15, ((0, 32),), jnp.float32)
    far_coupling = noise(keys[2], (BLOCKS, FAR, RANK, RANK), 0.025, 0.15, ((0, 32),), jnp.float32)
    leaf_basis = draw_leaf_basis(jax.random.fold_in(keys[7], 71), 0)
    parent_basis = draw_parent_basis(jax.random.fold_in(keys[7], 71), 0)
    near_index = draw_near_index(jax.random.fold_in(keys[7], 71), 0)
    far_index = draw_far_index(jax.random.fold_in(keys[7], 71), 0)
    return {"diag_block": diag_block, "near_blocks": near_blocks, "far_coupling": far_coupling, "leaf_basis": leaf_basis, "parent_basis": parent_basis, "near_index": near_index, "far_index": far_index}


precise_mode = lax.Precision.HIGHEST

def matmul(left_side, right_side):
    return jnp.dot(left_side, right_side, precision=precise_mode)

def sym_cholesky(square):
    return jnp.linalg.cholesky(0.5 * (square + square.T))

def lower_solve(triangle, right_side):
    return lax.linalg.triangular_solve(triangle, right_side, left_side=True, lower=True)

def leaf_eliminate(diag_one, basis_one):
    transformed = matmul(matmul(basis_one.T, diag_one), basis_one)
    leaf_low = sym_cholesky(transformed[:REDUN, :REDUN])
    coupled = lower_solve(leaf_low, transformed[:REDUN, REDUN:])
    leaf_schur = transformed[REDUN:, REDUN:] - matmul(coupled.T, coupled)
    return (jnp.concatenate([leaf_low, coupled], axis=1), leaf_schur)

def reference(diag_block, near_blocks, far_coupling, leaf_basis, parent_basis, near_index, far_index):
    skel_all = leaf_basis[:, :, REDUN:]
    bases = parent_basis.reshape(PARENTS, PAR, PAR)
    prev_skel = jnp.roll(bases, 1, axis=0)[:, :, PRED:]
    next_skel = jnp.roll(bases, -1, axis=0)[:, :, PRED:]
    leaf_ids = jnp.arange(BLOCKS, dtype=jnp.int32).reshape(PARENTS, GROUP)
    columns = jnp.arange(3 * GROUP, dtype=jnp.int32)

    def per_parent(packed):
        diag_group, near_group, far_group, basis_group, near_ids, far_ids, own_ids, parent_q, prev_q, next_q = packed
        factors, schur_all = jax.vmap(leaf_eliminate)(diag_group, basis_group)
        skel_own = basis_group[:, :, REDUN:]
        skeleton_near_block = jnp.take(skel_all, near_ids, axis=0)
        left_side_product = jnp.einsum('gar,gmac->gmrc', skel_own, near_group, precision=precise_mode)
        near_summands = jnp.einsum('yeiv,yevf->yeif', left_side_product, skeleton_near_block, precision=precise_mode)
        start = GROUP * (own_ids[0] // GROUP - 1)
        near_hot = (((near_ids - start) % BLOCKS)[..., None] == columns).astype(jnp.float32)
        far_hot = (((far_ids - start) % BLOCKS)[..., None] == columns).astype(jnp.float32)
        self_hot = ((GROUP + own_ids % GROUP)[:, None] == columns).astype(jnp.float32)
        window_blocks = jnp.einsum('gmc,gmab->gcab', near_hot, near_summands, precision=precise_mode)
        window_blocks = window_blocks + jnp.einsum('gmc,gmab->gcab', far_hot, far_group, precision=precise_mode)
        window_blocks = window_blocks + self_hot[:, :, None, None] * schur_all[:, None]
        hfull = jnp.transpose(window_blocks, (0, 2, 1, 3)).reshape(PAR, 3 * PAR)
        c_self = matmul(parent_q.T, matmul(hfull[:, PAR:2 * PAR], parent_q))
        c_prev = matmul(parent_q.T, matmul(hfull[:, :PAR], prev_q))
        c_next = matmul(parent_q.T, matmul(hfull[:, 2 * PAR:], next_q))
        parent_low = sym_cholesky(c_self[:PRED, :PRED])
        parent_coupled = lower_solve(parent_low, c_self[:PRED, PRED:])
        parent_trans = lower_solve(parent_low, c_self[PRED:, :PRED].T)
        parent_schur = c_self[PRED:, PRED:] - matmul(parent_trans.T, parent_coupled)
        factor_all = jnp.concatenate([parent_low, parent_coupled.T], axis=0)
        edge_block = jnp.concatenate([c_self[:PRED, PRED:], parent_schur], axis=0)
        coupling_all = jnp.concatenate([c_prev, edge_block, c_next], axis=1)
        return (factors, factor_all, coupling_all)
    packed_inputs = (diag_block.reshape(PARENTS, GROUP, LEAF, LEAF), near_blocks.reshape(PARENTS, GROUP, NEAR, LEAF, LEAF), far_coupling.reshape(PARENTS, GROUP, FAR, RANK, RANK), leaf_basis.reshape(PARENTS, GROUP, LEAF, LEAF), near_index.reshape(PARENTS, GROUP, NEAR), far_index.reshape(PARENTS, GROUP, FAR), leaf_ids, bases, prev_skel, next_skel)
    factors, parent_factors, couplings = lax.map(per_parent, packed_inputs)
    return (factors.reshape(BLOCKS * REDUN, LEAF), parent_factors.reshape(PARENTS * PAR, PRED), couplings.reshape(PARENTS * PAR, 3 * RANK))
```

```python
import functools

import jax
import jax.numpy as jnp
from jax import lax
from jax.experimental import pallas as pl
from jax.experimental.pallas import tpu as pltpu
from jax.sharding import PartitionSpec as P

LEAF = 512
RANK = 256
NEAR = 6
GROUP = 4
REDUN = 256
PAR = 1024
PRED = 768
FAR = 5
TILE = 128
ROWS = 8
WIDE = PRED + 2 * RANK

VMEM_BYTES = 56 * 1024 * 1024

NN = (((1,), (0,)), ((), ()))
TN = (((0,), (0,)), ((), ()))


def params():
    return pltpu.CompilerParams(vmem_limit_bytes=VMEM_BYTES)


def in_vmem():
    return pl.BlockSpec(memory_space=pltpu.VMEM)


def in_smem():
    return pl.BlockSpec(memory_space=pltpu.SMEM)


def split(value):
    high = value.astype(jnp.bfloat16)
    low = (value - high.astype(jnp.float32)).astype(jnp.bfloat16)
    return high, low


def dot3(left, right, dims=NN):
    def one(a, b):
        return lax.dot_general(a, b, dims, preferred_element_type=jnp.float32)

    return one(left[0], right[0]) + (one(left[0], right[1]) + one(left[1], right[0]))


def lane_spread(value, lane):
    return jnp.broadcast_to(value[:, lane : lane + 1], (ROWS, TILE))


def row_spread(value, row):
    return jnp.broadcast_to(value[row : row + 1, :], value.shape)


def panel_rows(parts, lane):
    sub = lax.broadcasted_iota(jnp.int32, (ROWS, TILE), 0)
    cols = [lane_spread(parts[0], lane + j) for j in range(ROWS)]
    parts = list(parts)
    scale = jnp.zeros((ROWS, TILE), jnp.float32)
    for j in range(ROWS):
        root = lax.rsqrt(row_spread(cols[j], j))
        scale = jnp.where(sub == j, root, scale)
        if j < ROWS - 1:
            factor = jnp.where(sub > j, cols[j] * (root * root), 0.0)
            for k in range(j + 1, ROWS):
                cols[k] = cols[k] - factor * row_spread(cols[k], j)
            parts = [part - factor * row_spread(part, j) for part in parts]
    return [part * scale for part in parts]


def tile_factor(square):
    count = TILE // ROWS
    row = lax.broadcasted_iota(jnp.int32, (ROWS, TILE), 0)
    col = lax.broadcasted_iota(jnp.int32, (ROWS, TILE), 1)
    left = [square[ROWS * i : ROWS * (i + 1), :] for i in range(count)]
    right = [jnp.where(row + ROWS * i == col, 1.0, 0.0).astype(jnp.float32) for i in range(count)]
    upper = []
    inverse = []
    pad1 = jnp.zeros((ROWS, TILE), jnp.float32)
    pad2 = jnp.zeros((ROWS, 2 * TILE), jnp.float32)
    for k in range(count):
        u_rows, m_rows = panel_rows([left[k], right[k]], ROWS * k)
        u_rows = jnp.where(col >= row + ROWS * k, u_rows, 0.0)
        upper.append(u_rows)
        inverse.append(m_rows)
        if k == count - 1:
            break
        both = jnp.concatenate([u_rows, m_rows], axis=1)
        high = both.astype(jnp.bfloat16).astype(jnp.float32)
        low = both - high
        lhs = jnp.concatenate([high[:, :TILE], high[:, :TILE], low[:, :TILE], pad1], axis=0)
        rhs = jnp.concatenate([high, low, high, pad2], axis=0)
        update = lax.dot_general(
            lhs.astype(jnp.bfloat16),
            rhs.astype(jnp.bfloat16),
            TN,
            preferred_element_type=jnp.float32,
        )
        for i in range(k + 1, count):
            rows = slice(ROWS * i, ROWS * (i + 1))
            left[i] = left[i] - update[rows, :TILE]
            right[i] = right[i] - update[rows, TILE:]
    return jnp.concatenate(upper, axis=0), jnp.concatenate(inverse, axis=0)


def leaf_kernel(diag_ref, basis_ref, out_ref, schur_ref, work, u_tile, m_tile):
    basis = split(basis_ref[...])
    half = split(dot3(split(diag_ref[...]), basis))
    redundant = [part[:, :REDUN] for part in basis]
    skeleton = [part[:, REDUN:] for part in basis]
    top = dot3(redundant, half, TN)
    square = top[:, :REDUN]
    work[:, :REDUN] = 0.5 * (square + square.T)
    work[:, REDUN:] = top[:, REDUN:]
    schur_ref[...] = dot3(skeleton, [part[:, REDUN:] for part in half], TN)

    def step(k, carry):
        rows = pl.ds(pl.multiple_of(k * TILE, TILE), TILE)
        upper, inverse = tile_factor(work[rows, rows])
        u_tile[...] = upper
        m_tile[...] = inverse
        new_rows = dot3(split(m_tile[...]), split(work[rows, :]))
        work[rows, :] = new_rows
        work[rows, rows] = u_tile[...]

        @pl.when(k == 0)
        def _():
            parts = split(new_rows)
            side = [part[:, TILE:REDUN] for part in parts]
            work[TILE:, TILE:] = work[TILE:, TILE:] - dot3(side, [part[:, TILE:] for part in parts], TN)

        return carry

    lax.fori_loop(0, REDUN // TILE, step, 0)
    row = lax.broadcasted_iota(jnp.int32, (REDUN, REDUN), 0)
    col = lax.broadcasted_iota(jnp.int32, (REDUN, REDUN), 1)
    out_ref[:, :REDUN] = jnp.where(row <= col, work[:, :REDUN], 0.0).T
    coupled = work[:, REDUN:]
    out_ref[:, REDUN:] = coupled
    parts = split(coupled)
    schur_ref[...] = schur_ref[...] - dot3(parts, parts, TN)


def left_kernel(skel_ref, near_ref, high_ref, low_ref):
    product = dot3(split(skel_ref[...]), split(near_ref[0]), TN)
    high, low = split(product)
    high_ref[0] = high
    low_ref[0] = low


def source_of(leaf, near_ref, far_ref):
    slot = jnp.int32(0)
    for m in range(NEAR):
        slot = slot + jnp.where(near_ref[0, m] == leaf, m, 0)
    for f in range(FAR):
        slot = slot + jnp.where(far_ref[0, f] == leaf, NEAR + f, 0)
    return slot


def window_block(leaf, near_ref, far_ref, high_ref, low_ref, far_blocks_ref, skel, put):
    slot = source_of(leaf, near_ref, far_ref)

    @pl.when(slot < NEAR)
    def _():
        m = jnp.minimum(slot, NEAR - 1)
        put(dot3((high_ref[m], low_ref[m]), split(skel[...])))

    @pl.when(slot >= NEAR)
    def _():
        f = jnp.clip(slot - NEAR, 0, FAR - 1)
        put(far_blocks_ref[f])


def own_kernel(me_ref, near_ref, far_ref, high_ref, low_ref, far_blocks_ref, s1, s2, s3, out_ref):
    for s, skel in enumerate((s1, s2, s3)):

        def put(block, s=s):
            out_ref[s] = block

        leaf = jnp.bitwise_xor(me_ref[0], s + 1)
        window_block(leaf, near_ref, far_ref, high_ref, low_ref, far_blocks_ref, skel, put)


def side_kernel(blocks, me_ref, near_ref, far_ref, high_ref, low_ref, far_blocks_ref, *rest):
    zs, (out_ref, held) = rest[:8], rest[8:]

    def put(block):
        held[...] = block

    for side, shift in enumerate((blocks - GROUP, GROUP)):
        for s in range(GROUP):
            z_ref = zs[side * GROUP + s]
            leaf = lax.rem(jnp.bitwise_xor(me_ref[0], s) + shift, blocks)
            window_block(
                leaf, near_ref, far_ref, high_ref, low_ref, far_blocks_ref, z_ref.at[:LEAF, :], put
            )
            term = dot3(split(held[...]), split(z_ref[LEAF:, :]))
            cols = slice(side * RANK, (side + 1) * RANK)
            if s == 0:
                out_ref[:, cols] = term
            else:
                out_ref[:, cols] = out_ref[:, cols] + term


def parent_kernel(me_ref, *rest):
    bases, hs, schurs = rest[:4], rest[4:8], rest[8:12]
    factor_ref, edge_ref = rest[12:14]
    p_high, p_low, v_high, v_low, whole, work, u_tile, m_tile = rest[14:]
    member = lax.rem(me_ref[0], GROUP)
    for s in range(GROUP):
        rows = slice(s * RANK, (s + 1) * RANK)
        high, low = split(bases[s][...])
        p_high[rows, :] = high
        p_low[rows, :] = low
    for s in range(GROUP):
        rows = slice(s * RANK, (s + 1) * RANK)
        line = [schurs[s][...] if t == s else hs[s][(s ^ t) - 1] for t in range(GROUP)]
        line = split(jnp.concatenate(line, axis=1))
        high, low = split(dot3(line, (p_high[...], p_low[...])))
        v_high[rows, :] = high
        v_low[rows, :] = low
    for m in range(GROUP):
        rows = slice(m * RANK, (m + 1) * RANK)
        whole[rows, :] = dot3((p_high[:, rows], p_low[:, rows]), (v_high[...], v_low[...]), TN)
    square = whole[:PRED, :PRED]
    work[:, :PRED] = 0.5 * (square + square.T)
    work[:, PRED:PAR] = whole[:PRED, PRED:]
    work[:, PAR:] = whole[PRED:, :PRED].T

    def step(k, carry):
        rows = pl.ds(pl.multiple_of(k * TILE, TILE), TILE)
        upper, inverse = tile_factor(work[rows, rows])
        u_tile[...] = upper
        m_tile[...] = inverse
        new_rows = dot3(split(m_tile[...]), split(work[rows, :]))
        work[rows, :] = new_rows
        work[rows, rows] = u_tile[...]
        parts = split(new_rows)
        for i in range(1, PRED // TILE):

            @pl.when(i > k)
            def _(i=i):
                below = slice(i * TILE, (i + 1) * TILE)
                side = [part[:, below] for part in parts]
                right = [part[:, i * TILE :] for part in parts]
                work[below, i * TILE :] = work[below, i * TILE :] - dot3(side, right, TN)

        return carry

    lax.fori_loop(0, PRED // TILE, step, 0)
    row = lax.broadcasted_iota(jnp.int32, (PRED, RANK), 0)
    col = lax.broadcasted_iota(jnp.int32, (PRED, RANK), 1) + member * RANK
    slab = pl.ds(pl.multiple_of(member * RANK, RANK), RANK)
    factor_ref[...] = jnp.where(row <= col, work[:, slab], 0.0).T
    edge_ref[...] = whole[slab, PRED:]

    @pl.when(member == GROUP - 1)
    def _():
        product = dot3(split(work[:, PAR:]), split(work[:, PRED:PAR]), TN)
        edge_ref[...] = whole[PRED:, PRED:] - product


def couple_kernel(me_ref, p0, p1, p2, p3, v0, v1, v2, v3, edge_ref, out_ref):
    member = lax.rem(me_ref[0], GROUP)
    slab = pl.ds(pl.multiple_of(member * RANK, RANK), RANK)
    total = jnp.zeros((RANK, 2 * RANK), jnp.float32)
    for p_ref, v_ref in ((p0, v0), (p1, v1), (p2, v2), (p3, v3)):
        total = total + dot3(split(p_ref[:, slab]), split(v_ref[...]), TN)
    out_ref[:, :RANK] = total[:, :RANK]
    out_ref[:, RANK : 2 * RANK] = edge_ref[...]
    out_ref[:, 2 * RANK :] = total[:, RANK:]


def swapped(value, axis, mask):
    pairs = [(source, source ^ mask) for source in range(lax.axis_size(axis))]
    return lax.ppermute(value, axis, pairs)


def shifted(value, axis, steps):
    count = lax.axis_size(axis)
    pairs = [(source, (source + steps) % count) for source in range(count)]
    return lax.ppermute(value, axis, pairs)


def gathered(value, axis):
    core = swapped(value, axis, 1)
    chip = swapped(value, axis, 2)
    both = swapped(chip, axis, 1)
    return [value, core, chip, both]


def on_device(
    diag_block, near_blocks, far_coupling, leaf_basis, parent_basis, near_index, far_index
):
    blocks = lax.axis_size("blk")
    me = lax.axis_index("blk").astype(jnp.int32).reshape(1)
    basis = leaf_basis[0]
    skeleton = basis[:, REDUN:]
    near = near_blocks[0]
    far = far_coupling[0]
    f32 = jnp.float32

    skels = gathered(skeleton, "blk")
    bases = gathered(parent_basis, "blk")
    load = jnp.concatenate([skeleton, parent_basis[:, PRED:]], axis=0)
    from_prev = gathered(shifted(load, "blk", GROUP), "blk")
    from_next = gathered(shifted(load, "blk", -GROUP), "blk")

    left_high, left_low = pl.pallas_call(
        left_kernel,
        grid=(NEAR,),
        in_specs=[
            pl.BlockSpec((LEAF, RANK), lambda m: (0, 1)),
            pl.BlockSpec((1, LEAF, LEAF), lambda m: (m, 0, 0)),
        ],
        out_specs=[pl.BlockSpec((1, RANK, LEAF), lambda m: (m, 0, 0))] * 2,
        out_shape=[jax.ShapeDtypeStruct((NEAR, RANK, LEAF), jnp.bfloat16)] * 2,
        compiler_params=params(),
        name="left_products",
    )(basis, near)

    leaf_out, leaf_schur = pl.pallas_call(
        leaf_kernel,
        in_specs=[in_vmem()] * 2,
        out_specs=[in_vmem()] * 2,
        out_shape=[
            jax.ShapeDtypeStruct((REDUN, LEAF), f32),
            jax.ShapeDtypeStruct((RANK, RANK), f32),
        ],
        scratch_shapes=[
            pltpu.VMEM((REDUN, LEAF), f32),
            pltpu.VMEM((TILE, TILE), f32),
            pltpu.VMEM((TILE, TILE), f32),
        ],
        compiler_params=params(),
        name="leaf_factor",
    )(diag_block[0], basis)

    own = pl.pallas_call(
        own_kernel,
        in_specs=[in_smem()] * 3 + [in_vmem()] * 6,
        out_specs=in_vmem(),
        out_shape=jax.ShapeDtypeStruct((GROUP - 1, RANK, RANK), f32),
        compiler_params=params(),
        name="own_window",
    )(me, near_index, far_index, left_high, left_low, far, *skels[1:])

    owns = gathered(own, "blk")
    schurs = gathered(leaf_schur, "blk")

    factor_rows, edge_rows = pl.pallas_call(
        parent_kernel,
        in_specs=[in_smem()] + [in_vmem()] * 12,
        out_specs=[in_vmem()] * 2,
        out_shape=[
            jax.ShapeDtypeStruct((RANK, PRED), f32),
            jax.ShapeDtypeStruct((RANK, RANK), f32),
        ],
        scratch_shapes=[pltpu.VMEM((PAR, PAR), jnp.bfloat16)] * 4
        + [
            pltpu.VMEM((PAR, PAR), f32),
            pltpu.VMEM((PRED, WIDE), f32),
            pltpu.VMEM((TILE, TILE), f32),
            pltpu.VMEM((TILE, TILE), f32),
        ],
        compiler_params=params(),
        name="parent_factor",
    )(me, *bases, *owns, *schurs)

    side = pl.pallas_call(
        functools.partial(side_kernel, blocks),
        in_specs=[in_smem()] * 3 + [in_vmem()] * 11,
        out_specs=in_vmem(),
        out_shape=jax.ShapeDtypeStruct((RANK, 2 * RANK), f32),
        scratch_shapes=[pltpu.VMEM((RANK, RANK), f32)],
        compiler_params=params(),
        name="side_windows",
    )(me, near_index, far_index, left_high, left_low, far, *from_prev, *from_next)
    sides = gathered(side, "blk")

    coupling_rows = pl.pallas_call(
        couple_kernel,
        in_specs=[in_smem()] + [in_vmem()] * 9,
        out_specs=in_vmem(),
        out_shape=jax.ShapeDtypeStruct((RANK, 3 * RANK), f32),
        compiler_params=params(),
        name="coupling",
    )(me, *bases, *sides, edge_rows)
    return (leaf_out, factor_rows, coupling_rows)


def solution(mesh):
    placed = (
        P("blk", None, None),
        P("blk", None, None, None),
        P("blk", None, None, None),
        P("blk", None, None),
        P("blk", None),
        P("blk", None),
        P("blk", None),
    )
    return jax.shard_map(
        on_device,
        mesh=mesh,
        in_specs=placed,
        out_specs=(P("blk", None), P("blk", None), P("blk", None)),
        check_vma=False,
    )
```

```python
import functools

import jax
import jax.numpy as jnp
from jax import lax
from jax.experimental import pallas as pl
from jax.experimental.pallas import tpu as pltpu
from jax.sharding import PartitionSpec as P

LEAF = 512
RANK = 256
NEAR = 6
GROUP = 4
REDUN = 256
PAR = 1024
PRED = 768
FAR = 5
TILE = 128
ROWS = 8
WIDE = PRED + 2 * RANK
EARLY = 4
MIDDLE = 30_000_000_000

VMEM_BYTES = 56 * 1024 * 1024

NN = (((1,), (0,)), ((), ()))
TN = (((0,), (0,)), ((), ()))


def params():
    return pltpu.CompilerParams(vmem_limit_bytes=VMEM_BYTES)


def in_vmem():
    return pl.BlockSpec(memory_space=pltpu.VMEM)


def in_smem():
    return pl.BlockSpec(memory_space=pltpu.SMEM)


def split(value):
    high = value.astype(jnp.bfloat16)
    low = (value - high.astype(jnp.float32)).astype(jnp.bfloat16)
    return high, low


def dot3(left, right, dims=NN):
    def one(a, b):
        return lax.dot_general(a, b, dims, preferred_element_type=jnp.float32)

    return one(left[0], right[0]) + (one(left[0], right[1]) + one(left[1], right[0]))


def lane_spread(value, lane):
    return jnp.broadcast_to(value[:, lane : lane + 1], (ROWS, TILE))


def row_spread(value, row):
    return jnp.broadcast_to(value[row : row + 1, :], (ROWS, TILE))


def small_inverse(entry):
    entry = dict(entry)
    low = {}
    inv = {}
    for j in range(ROWS):
        root = lax.rsqrt(entry[j, j])
        for i in range(j + 1, ROWS):
            low[i, j] = entry[i, j] * root
        for k in range(j + 1, ROWS):
            for i in range(k, ROWS):
                entry[i, k] = entry[i, k] - low[i, j] * low[k, j]
        inv[j, j] = root
        for t in range(j):
            total = low[j, t] * inv[t, t]
            for k in range(t + 1, j):
                total = total + low[j, k] * inv[k, t]
            inv[j, t] = -(total * root)
    return inv


def weighted(inv, j, values):
    total = inv[j, 0] * values[0]
    for t in range(1, j + 1):
        total = total + inv[j, t] * values[t]
    return total


def tile_factor(square):
    count = TILE // ROWS
    row = lax.broadcasted_iota(jnp.int32, (ROWS, TILE), 0)
    col = lax.broadcasted_iota(jnp.int32, (ROWS, TILE), 1)
    left = [square[ROWS * i : ROWS * (i + 1), :] for i in range(count)]
    right = [jnp.where(row + ROWS * i == col, 1.0, 0.0).astype(jnp.float32) for i in range(count)]
    upper = []
    inverse = []
    pad1 = jnp.zeros((ROWS, TILE), jnp.float32)
    pad2 = jnp.zeros((ROWS, 2 * TILE), jnp.float32)
    for k in range(count):
        cols = [lane_spread(left[k], ROWS * k + j) for j in range(ROWS)]
        inv = small_inverse(
            {(i, j): row_spread(cols[j], i) for j in range(ROWS) for i in range(j, ROWS)}
        )
        left_rows = [row_spread(left[k], t) for t in range(ROWS)]
        right_rows = [row_spread(right[k], t) for t in range(ROWS)]
        u_rows = m_rows = None
        for j in range(ROWS):
            weight = inv[ROWS - 1, j]
            for i in range(ROWS - 2, j - 1, -1):
                weight = jnp.where(row == i, inv[i, j], weight)
            if j > 0:
                weight = jnp.where(row >= j, weight, 0.0)
            u_term, m_term = weight * left_rows[j], weight * right_rows[j]
            u_rows = u_term if u_rows is None else u_rows + u_term
            m_rows = m_term if m_rows is None else m_rows + m_term
        u_rows = jnp.where(col >= row + ROWS * k, u_rows, 0.0)
        upper.append(u_rows)
        inverse.append(m_rows)
        if k == count - 1:
            break
        raw = [lane_spread(left[k + 1], ROWS * k + t) for t in range(ROWS)]
        u_total = m_total = None
        for j in range(ROWS):
            side = weighted(inv, j, raw)
            u_term = side * weighted(inv, j, left_rows)
            m_term = side * row_spread(m_rows, j)
            u_total = u_term if u_total is None else u_total + u_term
            m_total = m_term if m_total is None else m_total + m_term
        left[k + 1] = left[k + 1] - u_total
        right[k + 1] = right[k + 1] - m_total
        if k == count - 2:
            continue
        both = jnp.concatenate([u_rows, m_rows], axis=1)
        high = both.astype(jnp.bfloat16).astype(jnp.float32)
        low = both - high
        lhs = jnp.concatenate([high[:, :TILE], high[:, :TILE], low[:, :TILE], pad1], axis=0)
        rhs = jnp.concatenate([high, low, high, pad2], axis=0)
        update = lax.dot_general(
            lhs.astype(jnp.bfloat16),
            rhs.astype(jnp.bfloat16),
            TN,
            preferred_element_type=jnp.float32,
        )
        for i in range(k + 2, count):
            rows = slice(ROWS * i, ROWS * (i + 1))
            left[i] = left[i] - update[rows, :TILE]
            right[i] = right[i] - update[rows, TILE:]
    return jnp.concatenate(upper, axis=0), jnp.concatenate(inverse, axis=0)


def leaf_kernel(diag_ref, basis_ref, after1, out_ref, schur_ref, work, u_tile, m_tile):
    basis = split(basis_ref[...])
    half = split(dot3(split(diag_ref[...]), basis))
    redundant = [part[:, :REDUN] for part in basis]
    skeleton = [part[:, REDUN:] for part in basis]
    top = dot3(redundant, half, TN)
    square = top[:, :REDUN]
    work[:, :REDUN] = 0.5 * (square + square.T)
    work[:, REDUN:] = top[:, REDUN:]
    schur_ref[...] = dot3(skeleton, [part[:, REDUN:] for part in half], TN)

    def step(k, carry):
        rows = pl.ds(pl.multiple_of(k * TILE, TILE), TILE)
        upper, inverse = tile_factor(work[rows, rows])
        u_tile[...] = upper
        m_tile[...] = inverse
        new_rows = dot3(split(m_tile[...]), split(work[rows, :]))
        work[rows, :] = new_rows
        work[rows, rows] = u_tile[...]

        @pl.when(k == 0)
        def _():
            parts = split(new_rows)
            side = [part[:, TILE:REDUN] for part in parts]
            work[TILE:, TILE:] = work[TILE:, TILE:] - dot3(side, [part[:, TILE:] for part in parts], TN)

        return carry

    lax.fori_loop(0, REDUN // TILE, step, 0)
    row = lax.broadcasted_iota(jnp.int32, (REDUN, REDUN), 0)
    col = lax.broadcasted_iota(jnp.int32, (REDUN, REDUN), 1)
    out_ref[:, :REDUN] = jnp.where(row <= col, work[:, :REDUN], 0.0).T
    coupled = work[:, REDUN:]
    out_ref[:, REDUN:] = coupled
    parts = split(coupled)
    schur_ref[...] = schur_ref[...] - dot3(parts, parts, TN)


def left_kernel(skel_ref, near_ref, after1, high_ref, low_ref, skel_high, skel_low):
    @pl.when(pl.program_id(0) == 0)
    def _():
        high, low = split(skel_ref[...].T)
        skel_high[...] = high
        skel_low[...] = low

    high, low = split(dot3((skel_high[...], skel_low[...]), split(near_ref[0])))
    high_ref[0] = high
    low_ref[0] = low


def source_of(leaf, near_ref, far_ref):
    slot = jnp.int32(0)
    for m in range(NEAR):
        slot = slot + jnp.where(near_ref[0, m] == leaf, m, 0)
    for f in range(FAR):
        slot = slot + jnp.where(far_ref[0, f] == leaf, NEAR + f, 0)
    return slot, jnp.minimum(slot, NEAR - 1), jnp.maximum(slot - NEAR, 0)


def sibling_slots(me_ref, near_ref, far_ref):
    return [source_of(jnp.bitwise_xor(me_ref[0], s), near_ref, far_ref) for s in range(1, GROUP)]


def sibling_kernel(me_ref, near_ref, far_ref, skel_ref, near_hbm, high_ref, low_ref, held, sems):
    slots = sibling_slots(me_ref, near_ref, far_ref)
    copies = [
        pltpu.make_async_copy(near_hbm.at[m], held.at[s], sems.at[s])
        for s, (_, m, _) in enumerate(slots)
    ]
    for copy in copies:
        copy.start()
    skel = split(skel_ref[...].T)
    for s in range(GROUP - 1):
        copies[s].wait()

        @pl.when(slots[s][0] < NEAR)
        def _(s=s):
            high, low = split(dot3(skel, split(held[s])))
            high_ref[s] = high
            low_ref[s] = low


def own_kernel(
    me_ref, near_ref, far_ref, high_ref, low_ref, far_hbm, schur_ref, s1, s2, s3, out_ref, sems
):
    slots = sibling_slots(me_ref, near_ref, far_ref)
    copies = [
        pltpu.make_async_copy(far_hbm.at[f], out_ref.at[s + 1], sems.at[s])
        for s, (_, _, f) in enumerate(slots)
    ]
    for copy in copies:
        copy.start()
    out_ref[0] = schur_ref[...]
    for s, sibling in enumerate((s1, s2, s3)):
        copies[s].wait()

        @pl.when(slots[s][0] < NEAR)
        def _(s=s, sibling=sibling):
            out_ref[s + 1] = dot3((high_ref[s], low_ref[s]), split(sibling[...]))


def side_kernel(blocks, me_ref, near_ref, far_ref, high_hbm, low_hbm, far_hbm, *rest):
    zs, (after1, out_ref, z_held, high_held, low_held, far_held, h_high, h_low, s_high, s_low, sems) = (
        rest[:8],
        rest[8:],
    )
    slots = []
    z_copies = []
    near_copies = []
    far_copies = []
    for side, shift in enumerate((blocks - GROUP, GROUP)):
        for s in range(GROUP):
            n = side * GROUP + s
            leaf = lax.rem(jnp.bitwise_xor(me_ref[0], s) + shift, blocks)
            slot, m, f = source_of(leaf, near_ref, far_ref)
            slots.append(slot)
            z_copies.append(pltpu.make_async_copy(zs[n], z_held.at[n], sems.at[0, n]))
            near_copies.append(
                [
                    pltpu.make_async_copy(high_hbm.at[m], high_held.at[n], sems.at[1, n]),
                    pltpu.make_async_copy(low_hbm.at[m], low_held.at[n], sems.at[2, n]),
                ]
            )
            far_copies.append(pltpu.make_async_copy(far_hbm.at[f], far_held.at[n], sems.at[1, n]))
    for n in range(2 * GROUP):
        z_copies[n].start()

        @pl.when(slots[n] < NEAR)
        def _(n=n):
            for copy in near_copies[n]:
                copy.start()

        @pl.when(slots[n] >= NEAR)
        def _(n=n):
            far_copies[n].start()

    for side in range(2):
        for s in range(GROUP):
            n = side * GROUP + s
            cols = slice(s * RANK, (s + 1) * RANK)
            z_copies[n].wait()

            @pl.when(slots[n] < NEAR)
            def _(n=n, cols=cols):
                for copy in near_copies[n]:
                    copy.wait()
                high, low = split(dot3((high_held[n], low_held[n]), split(z_held[n, :LEAF, :])))
                h_high[:, cols] = high
                h_low[:, cols] = low

            @pl.when(slots[n] >= NEAR)
            def _(n=n, cols=cols):
                far_copies[n].wait()
                high, low = split(far_held[n])
                h_high[:, cols] = high
                h_low[:, cols] = low

            high, low = split(z_held[n, LEAF:, :])
            s_high[cols, :] = high
            s_low[cols, :] = low
        out_ref[:, side * RANK : (side + 1) * RANK] = dot3(
            (h_high[...], h_low[...]), (s_high[...], s_low[...])
        )


def partial_sums(p_high, p_low, h_refs, first, v_high, v_low):
    for s in range(2):
        line = [h_refs[s][(first + s) ^ t] for t in range(GROUP)]
        line = split(jnp.concatenate(line, axis=1))
        high, low = split(dot3(line, (p_high[...], p_low[...])))
        rows = slice(s * RANK, (s + 1) * RANK)
        v_high[rows, :] = high
        v_low[rows, :] = low


def chip_kernel(
    me_ref, p0, p1, p2, p3, h0, h1, after1, p_high, p_low, t_high, t_low, part_ref, v_high, v_low
):
    member = lax.rem(me_ref[0], GROUP)
    slab = pl.ds(pl.multiple_of(member * RANK, RANK), RANK)
    for s, base in enumerate((p0, p1, p2, p3)):
        rows = slice(s * RANK, (s + 1) * RANK)
        high, low = split(base[...])
        p_high[rows, :] = high
        p_low[rows, :] = low
        high, low = split(base[:, slab].T)
        t_high[:, rows] = high
        t_low[:, rows] = low
    partial_sums(p_high, p_low, (h0, h1), 0, v_high, v_low)
    half = slice(0, 2 * RANK)
    for m in range(GROUP):
        cols = slice(m * RANK, (m + 1) * RANK)
        part_ref[cols, :] = dot3(
            (p_high[half, cols], p_low[half, cols]), (v_high[...], v_low[...]), TN
        )


def eliminate(work, u_tile, m_tile, first, last):
    def step(k, carry):
        rows = pl.ds(pl.multiple_of(k * TILE, TILE), TILE)
        upper, inverse = tile_factor(work[rows, rows])
        u_tile[...] = upper
        m_tile[...] = inverse
        new_rows = dot3(split(m_tile[...]), split(work[rows, :]))
        work[rows, :] = new_rows
        work[rows, rows] = u_tile[...]
        parts = split(new_rows)
        for i in range(first + 1, PRED // TILE):

            @pl.when(i > k)
            def _(i=i):
                below = slice(i * TILE, (i + 1) * TILE)
                side = [part[:, below] for part in parts]
                right = [part[:, i * TILE :] for part in parts]
                work[below, i * TILE :] = work[below, i * TILE :] - dot3(side, right, TN)

        return carry

    lax.fori_loop(first, last, step, 0)


def parent_kernel(
    me_ref, p_high, p_low, part_ref, h2, h3, work, edge_ref, v_high, v_low, whole, u_tile, m_tile
):
    member = lax.rem(me_ref[0], GROUP)
    partial_sums(p_high, p_low, (h2, h3), 2, v_high, v_low)
    half = slice(2 * RANK, PAR)
    for m in range(GROUP):
        cols = slice(m * RANK, (m + 1) * RANK)
        whole[cols, :] = part_ref[cols, :] + dot3(
            (p_high[half, cols], p_low[half, cols]), (v_high[...], v_low[...]), TN
        )
    square = whole[:PRED, :PRED]
    work[:, :PRED] = 0.5 * (square + square.T)
    work[:, PRED:PAR] = whole[:PRED, PRED:]
    work[:, PAR:] = whole[PRED:, :PRED].T
    slab = pl.ds(pl.multiple_of(member * RANK, RANK), RANK)
    edge_ref[...] = whole[slab, PRED:]
    eliminate(work, u_tile, m_tile, 0, EARLY)


def finish_kernel(me_ref, work_hbm, edge_in, after1, factor_ref, edge_ref, work, u_tile, m_tile, sems):
    member = lax.rem(me_ref[0], GROUP)
    done = EARLY * TILE
    open_rows = pltpu.make_async_copy(work_hbm.at[done:, :], work.at[done:, :], sems.at[0])
    held_rows = pltpu.make_async_copy(work_hbm.at[:done, :], work.at[:done, :], sems.at[1])
    open_rows.start()
    held_rows.start()
    open_rows.wait()
    eliminate(work, u_tile, m_tile, EARLY, PRED // TILE)
    held_rows.wait()
    row = lax.broadcasted_iota(jnp.int32, (PRED, RANK), 0)
    col = lax.broadcasted_iota(jnp.int32, (PRED, RANK), 1) + member * RANK
    slab = pl.ds(pl.multiple_of(member * RANK, RANK), RANK)
    factor_ref[...] = jnp.where(row <= col, work[:, slab], 0.0).T
    edge_ref[...] = edge_in[...]

    @pl.when(member == GROUP - 1)
    def _():
        product = dot3(split(work[:, PAR:]), split(work[:, PRED:PAR]), TN)
        edge_ref[...] = edge_in[...] - product


def couple_kernel(t_high, t_low, v0, v1, v2, v3, edge_ref, out_ref):
    total = jnp.zeros((RANK, 2 * RANK), jnp.float32)
    for s, v_ref in enumerate((v0, v1, v2, v3)):
        cols = slice(s * RANK, (s + 1) * RANK)
        total = total + dot3((t_high[:, cols], t_low[:, cols]), split(v_ref[...]))
    out_ref[:, :RANK] = total[:, :RANK]
    out_ref[:, RANK : 2 * RANK] = edge_ref[...]
    out_ref[:, 2 * RANK :] = total[:, RANK:]


def swapped(value, axis, mask):
    pairs = [(source, source ^ mask) for source in range(lax.axis_size(axis))]
    return lax.ppermute(value, axis, pairs)


def shifted(value, axis, steps):
    count = lax.axis_size(axis)
    pairs = [(source, (source + steps) % count) for source in range(count)]
    return lax.ppermute(value, axis, pairs)


def after(value, *earlier):
    return lax.optimization_barrier((value, *earlier))[0]


def gathered(value, axis, *earlier):
    core = swapped(value, axis, 1)
    chip = swapped(value, axis, 2)
    both = swapped(after(chip, *earlier), axis, 1)
    return [value, core, chip, both]


def call(kernel, name, ins, outs, scratch, *operands, flops=1):
    return pl.pallas_call(
        kernel,
        in_specs=ins,
        out_specs=[in_vmem()] * len(outs),
        out_shape=[jax.ShapeDtypeStruct(shape, dtype) for shape, dtype in outs],
        scratch_shapes=scratch,
        compiler_params=params(),
        cost_estimate=pl.CostEstimate(flops=flops, bytes_accessed=1, transcendentals=0),

        name=name,
    )(*operands)


def anywhere():
    return pl.BlockSpec(memory_space=pl.ANY)


def on_device(
    diag_block, near_blocks, far_coupling, leaf_basis, parent_basis, near_index, far_index
):
    blocks = lax.axis_size("blk")
    me = lax.axis_index("blk").astype(jnp.int32).reshape(1)
    basis = leaf_basis[0]
    skeleton = basis[:, REDUN:]
    near = near_blocks[0]
    far = far_coupling[0]
    f32, b16 = jnp.float32, jnp.bfloat16

    load = jnp.concatenate([skeleton, parent_basis[:, PRED:]], axis=0)
    prev_load = shifted(load, "blk", GROUP)
    next_load = shifted(load, "blk", -GROUP)

    base_chip = swapped(parent_basis, "blk", 2)

    sib_high, sib_low = call(
        sibling_kernel,
        "sibling_products",
        [in_smem()] * 3 + [in_vmem(), anywhere()],
        [((GROUP - 1, RANK, LEAF), b16)] * 2,
        [pltpu.VMEM((GROUP - 1, LEAF, LEAF), f32), pltpu.SemaphoreType.DMA((GROUP - 1,))],
        me,
        near_index,
        far_index,
        skeleton,
        near,
    )
    leaf_out, leaf_schur = call(
        leaf_kernel,
        "leaf_factor",
        [in_vmem()] * 2 + [anywhere()],
        [((REDUN, LEAF), f32), ((RANK, RANK), f32)],
        [pltpu.VMEM((REDUN, LEAF), f32), pltpu.VMEM((TILE, TILE), f32), pltpu.VMEM((TILE, TILE), f32)],
        diag_block[0],
        basis,
        sib_high,
        flops=MIDDLE,
    )
    skels = gathered(skeleton, "blk")
    (own,) = call(
        own_kernel,
        "own_window",
        [in_smem()] * 3 + [in_vmem()] * 2 + [anywhere()] + [in_vmem()] * 4,
        [((GROUP, RANK, RANK), f32)],
        [pltpu.SemaphoreType.DMA((GROUP - 1,))],
        me,
        near_index,
        far_index,
        sib_high,
        sib_low,
        far,
        leaf_schur,
        *skels[1:],
    )
    own_core = swapped(own, "blk", 1)
    own_chip = swapped(own, "blk", 2)
    base_core = swapped(after(parent_basis, own), "blk", 1)
    base_both = swapped(after(base_chip, own, prev_load, next_load), "blk", 1)
    bases = [parent_basis, base_core, base_chip, base_both]

    left_high, left_low = pl.pallas_call(
        left_kernel,
        grid=(NEAR,),
        in_specs=[
            pl.BlockSpec((LEAF, RANK), lambda m: (0, 1)),
            pl.BlockSpec((1, LEAF, LEAF), lambda m: (m, 0, 0)),
            anywhere(),
        ],
        out_specs=[pl.BlockSpec((1, RANK, LEAF), lambda m: (m, 0, 0))] * 2,
        out_shape=[jax.ShapeDtypeStruct((NEAR, RANK, LEAF), b16)] * 2,
        scratch_shapes=[pltpu.VMEM((RANK, LEAF), b16)] * 2,
        compiler_params=params(),
        cost_estimate=pl.CostEstimate(flops=1, bytes_accessed=1, transcendentals=0),

        name="left_products",
    )(basis, near, own)
    p_high, p_low, t_high, t_low, part = call(
        chip_kernel,
        "chip_sums",
        [in_smem()] + [in_vmem()] * 6 + [anywhere()],
        [((PAR, PAR), b16)] * 2 + [((RANK, PAR), b16)] * 2 + [((PAR, PAR), f32)],
        [pltpu.VMEM((2 * RANK, PAR), b16)] * 2,
        me,
        *bases,
        own,
        own_core,
        left_high,
    )
    own_both = swapped(after(own_chip, part), "blk", 1)
    prev_load = after(prev_load, own_chip)
    next_load = after(next_load, own_chip)
    tiles = [pltpu.VMEM((TILE, TILE), f32)] * 2
    work, edge_rows = call(
        parent_kernel,
        "parent_factor",
        [in_smem()] + [in_vmem()] * 5,
        [((PRED, WIDE), f32), ((RANK, RANK), f32)],
        [pltpu.VMEM((2 * RANK, PAR), b16)] * 2 + [pltpu.VMEM((PAR, PAR), f32)] + tiles,
        me,
        p_high,
        p_low,
        part,
        own_chip,
        own_both,
    )
    from_prev = gathered(prev_load, "blk", edge_rows)
    from_next = gathered(next_load, "blk", edge_rows)
    (side,) = call(
        functools.partial(side_kernel, blocks),
        "side_windows",
        [in_smem()] * 3 + [anywhere()] * 12,
        [((RANK, 2 * RANK), f32)],
        [
            pltpu.VMEM((2 * GROUP, LEAF + RANK, RANK), f32),
            pltpu.VMEM((2 * GROUP, RANK, LEAF), b16),
            pltpu.VMEM((2 * GROUP, RANK, LEAF), b16),
            pltpu.VMEM((2 * GROUP, RANK, RANK), f32),
            pltpu.VMEM((RANK, PAR), b16),
            pltpu.VMEM((RANK, PAR), b16),
            pltpu.VMEM((PAR, RANK), b16),
            pltpu.VMEM((PAR, RANK), b16),
            pltpu.SemaphoreType.DMA((3, 2 * GROUP)),
        ],
        me,
        near_index,
        far_index,
        left_high,
        left_low,
        far,
        *from_prev,
        *from_next,
        edge_rows,
    )
    factor_rows, edge_rows = call(
        finish_kernel,
        "parent_finish",
        [in_smem(), anywhere(), in_vmem(), anywhere()],
        [((RANK, PRED), f32), ((RANK, RANK), f32)],
        [pltpu.VMEM((PRED, WIDE), f32)] + tiles + [pltpu.SemaphoreType.DMA((2,))],
        me,
        work,
        edge_rows,
        side,
    )
    sides = gathered(side, "blk", edge_rows)
    (coupling_rows,) = call(
        couple_kernel,
        "coupling",
        [in_vmem()] * 7,
        [((RANK, 3 * RANK), f32)],
        [],
        t_high,
        t_low,
        *sides,
        edge_rows,
    )
    return (leaf_out, factor_rows, coupling_rows)


def solution(mesh):
    placed = (
        P("blk", None, None),
        P("blk", None, None, None),
        P("blk", None, None, None),
        P("blk", None, None),
        P("blk", None),
        P("blk", None),
        P("blk", None),
    )
    return jax.shard_map(
        on_device,
        mesh=mesh,
        in_specs=placed,
        out_specs=(P("blk", None), P("blk", None), P("blk", None)),
        check_vma=False,
    )
```

```python
import functools

import jax
import jax.numpy as jnp
from jax import lax
from jax.experimental import pallas as pl
from jax.experimental.pallas import tpu as pltpu
from jax.sharding import PartitionSpec as P

LEAF = 512
RANK = 256
NEAR = 6
GROUP = 4
REDUN = 256
PAR = 1024
PRED = 768
FAR = 5
TILE = 128
ROWS = 8
WIDE = PRED + 2 * RANK
EARLY = 4
AHEAD = 2
MIDDLE = 30_000_000_000

VMEM_BYTES = 56 * 1024 * 1024

NN = (((1,), (0,)), ((), ()))
TN = (((0,), (0,)), ((), ()))


def params():
    return pltpu.CompilerParams(vmem_limit_bytes=VMEM_BYTES)


def in_vmem():
    return pl.BlockSpec(memory_space=pltpu.VMEM)


def in_smem():
    return pl.BlockSpec(memory_space=pltpu.SMEM)


def split(value):
    high = value.astype(jnp.bfloat16)
    low = (value - high.astype(jnp.float32)).astype(jnp.bfloat16)
    return high, low


def dot3(left, right, dims=NN):
    def one(a, b):
        return lax.dot_general(a, b, dims, preferred_element_type=jnp.float32)

    return one(left[0], right[0]) + (one(left[0], right[1]) + one(left[1], right[0]))


def lane_spread(value, lane):
    return jnp.broadcast_to(value[:, lane : lane + 1], (ROWS, TILE))


def row_spread(value, row):
    return jnp.broadcast_to(value[row : row + 1, :], (ROWS, TILE))


def small_inverse(entry):
    entry = dict(entry)
    low = {}
    inv = {}
    for j in range(ROWS):
        root = lax.rsqrt(entry[j, j])
        for i in range(j + 1, ROWS):
            low[i, j] = entry[i, j] * root
        for k in range(j + 1, ROWS):
            for i in range(k, ROWS):
                entry[i, k] = entry[i, k] - low[i, j] * low[k, j]
        inv[j, j] = root
        for t in range(j):
            total = low[j, t] * inv[t, t]
            for k in range(t + 1, j):
                total = total + low[j, k] * inv[k, t]
            inv[j, t] = -(total * root)
    return inv


def weighted(inv, j, values):
    total = inv[j, 0] * values[0]
    for t in range(1, j + 1):
        total = total + inv[j, t] * values[t]
    return total


def added(terms):
    while len(terms) > 1:
        terms = [terms[i] + terms[i + 1] for i in range(0, len(terms), 2)]
    return terms[0]


def tile_factor(square):
    count = TILE // ROWS
    row = lax.broadcasted_iota(jnp.int32, (ROWS, TILE), 0)
    col = lax.broadcasted_iota(jnp.int32, (ROWS, TILE), 1)
    left = [square[ROWS * i : ROWS * (i + 1), :] for i in range(count)]
    right = [jnp.where(row + ROWS * i == col, 1.0, 0.0).astype(jnp.float32) for i in range(count)]
    upper = []
    inverse = []
    pad1 = jnp.zeros((ROWS, TILE), jnp.float32)
    pad2 = jnp.zeros((ROWS, 2 * TILE), jnp.float32)
    cols = [lane_spread(left[0], j) for j in range(ROWS)]
    for k in range(count):
        inv = small_inverse(
            {(i, j): row_spread(cols[j], i) for j in range(ROWS) for i in range(j, ROWS)}
        )
        soon = range(k + 1, min(k + 1 + AHEAD, count))
        sides = {}
        for i in soon:
            raw = [lane_spread(left[i], ROWS * k + t) for t in range(ROWS)]
            sides[i] = [weighted(inv, j, raw) for j in range(ROWS)]
        if k + 1 < count:
            side = sides[k + 1]
            cols = [
                lane_spread(left[k + 1], ROWS * (k + 1) + j)
                - added([side[t] * row_spread(side[t], j) for t in range(ROWS)])
                for j in range(ROWS)
            ]
        u_rows = m_rows = None
        for j in range(ROWS):
            weight = inv[ROWS - 1, j]
            for i in range(ROWS - 2, j - 1, -1):
                weight = jnp.where(row == i, inv[i, j], weight)
            if j > 0:
                weight = jnp.where(row >= j, weight, 0.0)
            u_term = weight * row_spread(left[k], j)
            m_term = weight * row_spread(right[k], j)
            u_rows = u_term if u_rows is None else u_rows + u_term
            m_rows = m_term if m_rows is None else m_rows + m_term
        u_rows = jnp.where(col >= row + ROWS * k, u_rows, 0.0)
        upper.append(u_rows)
        inverse.append(m_rows)
        for i in soon:
            left[i] = left[i] - added([sides[i][j] * row_spread(u_rows, j) for j in range(ROWS)])
            right[i] = right[i] - added([sides[i][j] * row_spread(m_rows, j) for j in range(ROWS)])
        if k + 1 + AHEAD >= count:
            continue
        both = jnp.concatenate([u_rows, m_rows], axis=1)
        high = both.astype(jnp.bfloat16).astype(jnp.float32)
        low = both - high
        lhs = jnp.concatenate([high[:, :TILE], high[:, :TILE], low[:, :TILE], pad1], axis=0)
        rhs = jnp.concatenate([high, low, high, pad2], axis=0)
        update = lax.dot_general(
            lhs.astype(jnp.bfloat16),
            rhs.astype(jnp.bfloat16),
            TN,
            preferred_element_type=jnp.float32,
        )
        for i in range(k + 1 + AHEAD, count):
            rows = slice(ROWS * i, ROWS * (i + 1))
            left[i] = left[i] - update[rows, :TILE]
            right[i] = right[i] - update[rows, TILE:]
    return jnp.concatenate(upper, axis=0), jnp.concatenate(inverse, axis=0)


def leaf_kernel(diag_ref, basis_ref, after1, out_ref, schur_ref, work, u_tile, m_tile):
    basis = split(basis_ref[...])
    half = split(dot3(split(diag_ref[...]), basis))
    redundant = [part[:, :REDUN] for part in basis]
    skeleton = [part[:, REDUN:] for part in basis]
    top = dot3(redundant, half, TN)
    square = top[:, :REDUN]
    work[:, :REDUN] = 0.5 * (square + square.T)
    work[:, REDUN:] = top[:, REDUN:]
    schur_ref[...] = dot3(skeleton, [part[:, REDUN:] for part in half], TN)

    def step(k, carry):
        rows = pl.ds(pl.multiple_of(k * TILE, TILE), TILE)
        upper, inverse = tile_factor(work[rows, rows])
        u_tile[...] = upper
        m_tile[...] = inverse
        new_rows = dot3(split(m_tile[...]), split(work[rows, :]))
        work[rows, :] = new_rows
        work[rows, rows] = u_tile[...]

        @pl.when(k == 0)
        def _():
            parts = split(new_rows)
            side = [part[:, TILE:REDUN] for part in parts]
            work[TILE:, TILE:] = work[TILE:, TILE:] - dot3(side, [part[:, TILE:] for part in parts], TN)

        return carry

    lax.fori_loop(0, REDUN // TILE, step, 0)
    row = lax.broadcasted_iota(jnp.int32, (REDUN, REDUN), 0)
    col = lax.broadcasted_iota(jnp.int32, (REDUN, REDUN), 1)
    out_ref[:, :REDUN] = jnp.where(row <= col, work[:, :REDUN], 0.0).T
    coupled = work[:, REDUN:]
    out_ref[:, REDUN:] = coupled
    parts = split(coupled)
    schur_ref[...] = schur_ref[...] - dot3(parts, parts, TN)


def left_kernel(skel_ref, near_ref, after1, high_ref, low_ref, skel_high, skel_low):
    @pl.when(pl.program_id(0) == 0)
    def _():
        high, low = split(skel_ref[...].T)
        skel_high[...] = high
        skel_low[...] = low

    high, low = split(dot3((skel_high[...], skel_low[...]), split(near_ref[0])))
    high_ref[0] = high
    low_ref[0] = low


def source_of(leaf, near_ref, far_ref):
    slot = jnp.int32(0)
    for m in range(NEAR):
        slot = slot + jnp.where(near_ref[0, m] == leaf, m, 0)
    for f in range(FAR):
        slot = slot + jnp.where(far_ref[0, f] == leaf, NEAR + f, 0)
    return slot, jnp.minimum(slot, NEAR - 1), jnp.maximum(slot - NEAR, 0)


def sibling_slots(me_ref, near_ref, far_ref):
    return [source_of(jnp.bitwise_xor(me_ref[0], s), near_ref, far_ref) for s in range(1, GROUP)]


def sibling_kernel(me_ref, near_ref, far_ref, skel_ref, near_hbm, high_ref, low_ref, held, sems):
    slots = sibling_slots(me_ref, near_ref, far_ref)
    copies = [
        pltpu.make_async_copy(near_hbm.at[m], held.at[s], sems.at[s])
        for s, (_, m, _) in enumerate(slots)
    ]
    for copy in copies:
        copy.start()
    skel = split(skel_ref[...].T)
    for s in range(GROUP - 1):
        copies[s].wait()

        @pl.when(slots[s][0] < NEAR)
        def _(s=s):
            high, low = split(dot3(skel, split(held[s])))
            high_ref[s] = high
            low_ref[s] = low


def block_rows(s):
    return slice(s * RANK, (s + 1) * RANK)


def own_kernel(
    me_ref, near_ref, far_ref, high_ref, low_ref, far_hbm, schur_ref, s1, s2, s3, out_ref, sems
):
    slots = sibling_slots(me_ref, near_ref, far_ref)
    copies = [
        pltpu.make_async_copy(far_hbm.at[f], out_ref.at[block_rows(s + 1), :], sems.at[s])
        for s, (_, _, f) in enumerate(slots)
    ]
    for copy in copies:
        copy.start()
    out_ref[block_rows(0), :] = schur_ref[...]
    out_ref[GROUP * RANK :, :] = jnp.zeros((ROWS, RANK), jnp.float32)
    for s, sibling in enumerate((s1, s2, s3)):
        copies[s].wait()

        @pl.when(slots[s][0] < NEAR)
        def _(s=s, sibling=sibling):
            out_ref[block_rows(s + 1), :] = dot3((high_ref[s], low_ref[s]), split(sibling[...]))


def side_kernel(blocks, me_ref, near_ref, far_ref, high_hbm, low_hbm, far_hbm, *rest):
    zs, (after1, out_ref, z_held, high_held, low_held, far_held, h_high, h_low, s_high, s_low, sems) = (
        rest[:8],
        rest[8:],
    )
    slots = []
    z_copies = []
    near_copies = []
    far_copies = []
    for side, shift in enumerate((blocks - GROUP, GROUP)):
        for s in range(GROUP):
            n = side * GROUP + s
            leaf = lax.rem(jnp.bitwise_xor(me_ref[0], s) + shift, blocks)
            slot, m, f = source_of(leaf, near_ref, far_ref)
            slots.append(slot)
            z_copies.append(pltpu.make_async_copy(zs[n], z_held.at[n], sems.at[0, n]))
            near_copies.append(
                [
                    pltpu.make_async_copy(high_hbm.at[m], high_held.at[n], sems.at[1, n]),
                    pltpu.make_async_copy(low_hbm.at[m], low_held.at[n], sems.at[2, n]),
                ]
            )
            far_copies.append(pltpu.make_async_copy(far_hbm.at[f], far_held.at[n], sems.at[1, n]))
    for n in range(2 * GROUP):
        z_copies[n].start()

        @pl.when(slots[n] < NEAR)
        def _(n=n):
            for copy in near_copies[n]:
                copy.start()

        @pl.when(slots[n] >= NEAR)
        def _(n=n):
            far_copies[n].start()

    for side in range(2):
        for s in range(GROUP):
            n = side * GROUP + s
            cols = slice(s * RANK, (s + 1) * RANK)
            z_copies[n].wait()

            @pl.when(slots[n] < NEAR)
            def _(n=n, cols=cols):
                for copy in near_copies[n]:
                    copy.wait()
                high, low = split(dot3((high_held[n], low_held[n]), split(z_held[n, :LEAF, :])))
                h_high[:, cols] = high
                h_low[:, cols] = low

            @pl.when(slots[n] >= NEAR)
            def _(n=n, cols=cols):
                far_copies[n].wait()
                high, low = split(far_held[n])
                h_high[:, cols] = high
                h_low[:, cols] = low

            high, low = split(z_held[n, LEAF:, :])
            s_high[cols, :] = high
            s_low[cols, :] = low
        out_ref[:, side * RANK : (side + 1) * RANK] = dot3(
            (h_high[...], h_low[...]), (s_high[...], s_low[...])
        )


def partial_sums(p_high, p_low, h_refs, first, v_high, v_low):
    for s in range(2):
        line = [h_refs[s][block_rows((first + s) ^ t), :] for t in range(GROUP)]
        line = split(jnp.concatenate(line, axis=1))
        high, low = split(dot3(line, (p_high[...], p_low[...])))
        rows = slice(s * RANK, (s + 1) * RANK)
        v_high[rows, :] = high
        v_low[rows, :] = low


def chip_kernel(
    me_ref, h0, h1, p0, p1, p2, p3, after1, p_high, p_low, t_high, t_low, part_ref, v_high, v_low
):
    member = lax.rem(me_ref[0], GROUP)
    slab = pl.ds(pl.multiple_of(member * RANK, RANK), RANK)
    for s, base in enumerate((p0, p1, p2, p3)):
        rows = slice(s * RANK, (s + 1) * RANK)
        high, low = split(base[...])
        p_high[rows, :] = high
        p_low[rows, :] = low
        high, low = split(base[:, slab].T)
        t_high[:, rows] = high
        t_low[:, rows] = low
    partial_sums(p_high, p_low, (h0, h1), 0, v_high, v_low)
    half = slice(0, 2 * RANK)
    for m in range(GROUP):
        cols = slice(m * RANK, (m + 1) * RANK)
        part_ref[cols, :] = dot3(
            (p_high[half, cols], p_low[half, cols]), (v_high[...], v_low[...]), TN
        )


def eliminate(work, u_tile, m_tile, first, last):
    def step(k, carry):
        rows = pl.ds(pl.multiple_of(k * TILE, TILE), TILE)
        upper, inverse = tile_factor(work[rows, rows])
        u_tile[...] = upper
        m_tile[...] = inverse
        new_rows = dot3(split(m_tile[...]), split(work[rows, :]))
        work[rows, :] = new_rows
        work[rows, rows] = u_tile[...]
        parts = split(new_rows)
        for i in range(first + 1, PRED // TILE):

            @pl.when(i > k)
            def _(i=i):
                below = slice(i * TILE, (i + 1) * TILE)
                side = [part[:, below] for part in parts]
                right = [part[:, i * TILE :] for part in parts]
                work[below, i * TILE :] = work[below, i * TILE :] - dot3(side, right, TN)

        return carry

    lax.fori_loop(first, last, step, 0)


def parent_kernel(
    me_ref, h2, h3, p_high, p_low, part_ref, work, edge_ref, v_high, v_low, whole, u_tile, m_tile
):
    member = lax.rem(me_ref[0], GROUP)
    partial_sums(p_high, p_low, (h2, h3), 2, v_high, v_low)
    half = slice(2 * RANK, PAR)
    for m in range(GROUP):
        cols = slice(m * RANK, (m + 1) * RANK)
        whole[cols, :] = part_ref[cols, :] + dot3(
            (p_high[half, cols], p_low[half, cols]), (v_high[...], v_low[...]), TN
        )
    square = whole[:PRED, :PRED]
    work[:, :PRED] = 0.5 * (square + square.T)
    work[:, PRED:PAR] = whole[:PRED, PRED:]
    work[:, PAR:] = whole[PRED:, :PRED].T
    slab = pl.ds(pl.multiple_of(member * RANK, RANK), RANK)
    edge_ref[...] = whole[slab, PRED:]
    eliminate(work, u_tile, m_tile, 0, EARLY)


def finish_kernel(me_ref, work_hbm, edge_in, after1, factor_ref, edge_ref, work, u_tile, m_tile, sems):
    member = lax.rem(me_ref[0], GROUP)
    done = EARLY * TILE
    open_rows = pltpu.make_async_copy(work_hbm.at[done:, :], work.at[done:, :], sems.at[0])
    held_rows = pltpu.make_async_copy(work_hbm.at[:done, :], work.at[:done, :], sems.at[1])
    open_rows.start()
    held_rows.start()
    open_rows.wait()
    eliminate(work, u_tile, m_tile, EARLY, PRED // TILE)
    held_rows.wait()
    row = lax.broadcasted_iota(jnp.int32, (PRED, RANK), 0)
    col = lax.broadcasted_iota(jnp.int32, (PRED, RANK), 1) + member * RANK
    slab = pl.ds(pl.multiple_of(member * RANK, RANK), RANK)
    factor_ref[...] = jnp.where(row <= col, work[:, slab], 0.0).T
    edge_ref[...] = edge_in[...]

    @pl.when(member == GROUP - 1)
    def _():
        product = dot3(split(work[:, PAR:]), split(work[:, PRED:PAR]), TN)
        edge_ref[...] = edge_in[...] - product


def couple_kernel(t_high, t_low, v0, v1, v2, v3, edge_ref, out_ref):
    total = jnp.zeros((RANK, 2 * RANK), jnp.float32)
    for s, v_ref in enumerate((v0, v1, v2, v3)):
        cols = slice(s * RANK, (s + 1) * RANK)
        total = total + dot3((t_high[:, cols], t_low[:, cols]), split(v_ref[...]))
    out_ref[:, :RANK] = total[:, :RANK]
    out_ref[:, RANK : 2 * RANK] = edge_ref[...]
    out_ref[:, 2 * RANK :] = total[:, RANK:]


def swapped(value, axis, mask):
    pairs = [(source, source ^ mask) for source in range(lax.axis_size(axis))]
    return lax.ppermute(value, axis, pairs)


def shifted(value, axis, steps):
    count = lax.axis_size(axis)
    pairs = [(source, (source + steps) % count) for source in range(count)]
    return lax.ppermute(value, axis, pairs)


def after(value, *earlier):
    return lax.optimization_barrier((value, *earlier))[0]


def gathered(value, axis, *earlier):
    core = swapped(value, axis, 1)
    chip = swapped(value, axis, 2)
    both = swapped(after(chip, *earlier), axis, 1)
    return [value, core, chip, both]


def call(kernel, name, ins, outs, scratch, *operands, flops=1):
    return pl.pallas_call(
        kernel,
        in_specs=ins,
        out_specs=[in_vmem()] * len(outs),
        out_shape=[jax.ShapeDtypeStruct(shape, dtype) for shape, dtype in outs],
        scratch_shapes=scratch,
        compiler_params=params(),
        cost_estimate=pl.CostEstimate(flops=flops, bytes_accessed=1, transcendentals=0),

        name=name,
    )(*operands)


def anywhere():
    return pl.BlockSpec(memory_space=pl.ANY)


def on_device(
    diag_block, near_blocks, far_coupling, leaf_basis, parent_basis, near_index, far_index
):
    blocks = lax.axis_size("blk")
    me = lax.axis_index("blk").astype(jnp.int32).reshape(1)
    basis = leaf_basis[0]
    skeleton = basis[:, REDUN:]
    near = near_blocks[0]
    far = far_coupling[0]
    f32, b16 = jnp.float32, jnp.bfloat16

    load = jnp.concatenate([skeleton, parent_basis[:, PRED:]], axis=0)
    prev_load = shifted(load, "blk", GROUP)
    next_load = shifted(load, "blk", -GROUP)

    base_chip = swapped(parent_basis, "blk", 2)

    sib_high, sib_low = call(
        sibling_kernel,
        "sibling_products",
        [in_smem()] * 3 + [in_vmem(), anywhere()],
        [((GROUP - 1, RANK, LEAF), b16)] * 2,
        [pltpu.VMEM((GROUP - 1, LEAF, LEAF), f32), pltpu.SemaphoreType.DMA((GROUP - 1,))],
        me,
        near_index,
        far_index,
        skeleton,
        near,
    )
    leaf_out, leaf_schur = call(
        leaf_kernel,
        "leaf_factor",
        [in_vmem()] * 2 + [anywhere()],
        [((REDUN, LEAF), f32), ((RANK, RANK), f32)],
        [pltpu.VMEM((REDUN, LEAF), f32), pltpu.VMEM((TILE, TILE), f32), pltpu.VMEM((TILE, TILE), f32)],
        diag_block[0],
        basis,
        sib_high,
        flops=MIDDLE,
    )
    skel_chip = swapped(skeleton, "blk", 2)
    skel_core = swapped(skeleton, "blk", 1)
    skels = [skeleton, skel_core, skel_chip, swapped(skel_chip, "blk", 1)]
    (own,) = call(
        own_kernel,
        "own_window",
        [in_smem()] * 3 + [in_vmem()] * 2 + [anywhere()] + [in_vmem()] * 4,
        [((GROUP * RANK + ROWS, RANK), f32)],
        [pltpu.SemaphoreType.DMA((GROUP - 1,))],
        me,
        near_index,
        far_index,
        sib_high,
        sib_low,
        far,
        leaf_schur,
        *skels[1:],
    )
    own_core = swapped(own, "blk", 1)
    own_chip = swapped(own, "blk", 2)

    left_high, left_low = pl.pallas_call(
        left_kernel,
        grid=(NEAR,),
        in_specs=[
            pl.BlockSpec((LEAF, RANK), lambda m: (0, 1)),
            pl.BlockSpec((1, LEAF, LEAF), lambda m: (m, 0, 0)),
            anywhere(),
        ],
        out_specs=[pl.BlockSpec((1, RANK, LEAF), lambda m: (m, 0, 0))] * 2,
        out_shape=[jax.ShapeDtypeStruct((NEAR, RANK, LEAF), b16)] * 2,
        scratch_shapes=[pltpu.VMEM((RANK, LEAF), b16)] * 2,
        compiler_params=params(),
        cost_estimate=pl.CostEstimate(flops=1, bytes_accessed=1, transcendentals=0),

        name="left_products",
    )(basis, near, own)
    base_core = swapped(after(parent_basis, left_high), "blk", 1)
    base_both = swapped(after(base_chip, left_high, prev_load, next_load), "blk", 1)
    bases = [parent_basis, base_core, base_chip, base_both]
    p_high, p_low, t_high, t_low, part = call(
        chip_kernel,
        "chip_sums",
        [in_smem()] + [in_vmem()] * 6 + [anywhere()],
        [((PAR, PAR), b16)] * 2 + [((RANK, PAR), b16)] * 2 + [((PAR, PAR), f32)],
        [pltpu.VMEM((2 * RANK, PAR), b16)] * 2,
        me,
        own,
        own_core,
        *bases,
        left_high,
    )
    own_both = swapped(after(own_chip, part), "blk", 1)
    prev_load = after(prev_load, own_chip)
    next_load = after(next_load, own_chip)
    tiles = [pltpu.VMEM((TILE, TILE), f32)] * 2
    work, edge_rows = call(
        parent_kernel,
        "parent_factor",
        [in_smem()] + [in_vmem()] * 5,
        [((PRED, WIDE), f32), ((RANK, RANK), f32)],
        [pltpu.VMEM((2 * RANK, PAR), b16)] * 2 + [pltpu.VMEM((PAR, PAR), f32)] + tiles,
        me,
        own_chip,
        own_both,
        p_high,
        p_low,
        part,
    )
    from_prev = gathered(prev_load, "blk", edge_rows)
    from_next = gathered(next_load, "blk", edge_rows)
    (side,) = call(
        functools.partial(side_kernel, blocks),
        "side_windows",
        [in_smem()] * 3 + [anywhere()] * 12,
        [((RANK, 2 * RANK), f32)],
        [
            pltpu.VMEM((2 * GROUP, LEAF + RANK, RANK), f32),
            pltpu.VMEM((2 * GROUP, RANK, LEAF), b16),
            pltpu.VMEM((2 * GROUP, RANK, LEAF), b16),
            pltpu.VMEM((2 * GROUP, RANK, RANK), f32),
            pltpu.VMEM((RANK, PAR), b16),
            pltpu.VMEM((RANK, PAR), b16),
            pltpu.VMEM((PAR, RANK), b16),
            pltpu.VMEM((PAR, RANK), b16),
            pltpu.SemaphoreType.DMA((3, 2 * GROUP)),
        ],
        me,
        near_index,
        far_index,
        left_high,
        left_low,
        far,
        *from_prev,
        *from_next,
        edge_rows,
    )
    factor_rows, edge_rows = call(
        finish_kernel,
        "parent_finish",
        [in_smem(), anywhere(), in_vmem(), anywhere()],
        [((RANK, PRED), f32), ((RANK, RANK), f32)],
        [pltpu.VMEM((PRED, WIDE), f32)] + tiles + [pltpu.SemaphoreType.DMA((2,))],
        me,
        work,
        edge_rows,
        side,
    )
    sides = gathered(side, "blk", edge_rows)
    (coupling_rows,) = call(
        couple_kernel,
        "coupling",
        [in_vmem()] * 7,
        [((RANK, 3 * RANK), f32)],
        [],
        t_high,
        t_low,
        *sides,
        edge_rows,
    )
    return (leaf_out, factor_rows, coupling_rows)


def solution(mesh):
    placed = (
        P("blk", None, None),
        P("blk", None, None, None),
        P("blk", None, None, None),
        P("blk", None, None),
        P("blk", None),
        P("blk", None),
        P("blk", None),
    )
    return jax.shard_map(
        on_device,
        mesh=mesh,
        in_specs=placed,
        out_specs=(P("blk", None), P("blk", None), P("blk", None)),
        check_vma=False,
    )
```

```python
import functools

import jax
import jax.numpy as jnp
from jax import lax
from jax.experimental import pallas as pl
from jax.experimental.pallas import tpu as pltpu
from jax.sharding import PartitionSpec as P

LEAF = 512
RANK = 256
NEAR = 6
GROUP = 4
REDUN = 256
PAR = 1024
PRED = 768
FAR = 5
TILE = 128
ROWS = 8
WIDE = PRED + 2 * RANK
EARLY = 4
AHEAD = 2
MIDDLE = 30_000_000_000

VMEM_BYTES = 64 * 1024 * 1024
VMEM_EARLY = 48 * 1024 * 1024

NN = (((1,), (0,)), ((), ()))
TN = (((0,), (0,)), ((), ()))


def params(limit=VMEM_BYTES):
    return pltpu.CompilerParams(vmem_limit_bytes=limit)


def in_vmem():
    return pl.BlockSpec(memory_space=pltpu.VMEM)


def in_smem():
    return pl.BlockSpec(memory_space=pltpu.SMEM)


def split(value):
    high = value.astype(jnp.bfloat16)
    low = (value - high.astype(jnp.float32)).astype(jnp.bfloat16)
    return high, low


def dot3(left, right, dims=NN):
    def one(a, b):
        return lax.dot_general(a, b, dims, preferred_element_type=jnp.float32)

    return one(left[0], right[0]) + (one(left[0], right[1]) + one(left[1], right[0]))


def lane_spread(value, lane):
    return jnp.broadcast_to(value[:, lane : lane + 1], (ROWS, TILE))


def row_spread(value, row):
    return jnp.broadcast_to(value[row : row + 1, :], (ROWS, TILE))


def small_inverse(entry):
    entry = dict(entry)
    low = {}
    inv = {}
    for j in range(ROWS):
        root = lax.rsqrt(entry[j, j])
        for i in range(j + 1, ROWS):
            low[i, j] = entry[i, j] * root
        for k in range(j + 1, ROWS):
            for i in range(k, ROWS):
                entry[i, k] = entry[i, k] - low[i, j] * low[k, j]
        inv[j, j] = root
        for t in range(j):
            total = low[j, t] * inv[t, t]
            for k in range(t + 1, j):
                total = total + low[j, k] * inv[k, t]
            inv[j, t] = -(total * root)
    return inv


def weighted(inv, j, values):
    total = inv[j, 0] * values[0]
    for t in range(1, j + 1):
        total = total + inv[j, t] * values[t]
    return total


def added(terms):
    while len(terms) > 1:
        terms = [terms[i] + terms[i + 1] for i in range(0, len(terms), 2)]
    return terms[0]


def tile_factor(square):
    count = TILE // ROWS
    row = lax.broadcasted_iota(jnp.int32, (ROWS, TILE), 0)
    col = lax.broadcasted_iota(jnp.int32, (ROWS, TILE), 1)
    left = [square[ROWS * i : ROWS * (i + 1), :] for i in range(count)]
    right = [jnp.where(row + ROWS * i == col, 1.0, 0.0).astype(jnp.float32) for i in range(count)]
    upper = []
    inverse = []
    pad1 = jnp.zeros((ROWS, TILE), jnp.float32)
    pad2 = jnp.zeros((ROWS, 2 * TILE), jnp.float32)
    cols = [lane_spread(left[0], j) for j in range(ROWS)]
    for k in range(count):
        inv = small_inverse(
            {(i, j): row_spread(cols[j], i) for j in range(ROWS) for i in range(j, ROWS)}
        )
        soon = range(k + 1, min(k + 1 + AHEAD, count))
        sides = {}
        for i in soon:
            raw = [lane_spread(left[i], ROWS * k + t) for t in range(ROWS)]
            sides[i] = [weighted(inv, j, raw) for j in range(ROWS)]
        if k + 1 < count:
            side = sides[k + 1]
            cols = [
                lane_spread(left[k + 1], ROWS * (k + 1) + j)
                - added([side[t] * row_spread(side[t], j) for t in range(ROWS)])
                for j in range(ROWS)
            ]
        u_rows = m_rows = None
        for j in range(ROWS):
            weight = inv[ROWS - 1, j]
            for i in range(ROWS - 2, j - 1, -1):
                weight = jnp.where(row == i, inv[i, j], weight)
            if j > 0:
                weight = jnp.where(row >= j, weight, 0.0)
            u_term = weight * row_spread(left[k], j)
            m_term = weight * row_spread(right[k], j)
            u_rows = u_term if u_rows is None else u_rows + u_term
            m_rows = m_term if m_rows is None else m_rows + m_term
        u_rows = jnp.where(col >= row + ROWS * k, u_rows, 0.0)
        upper.append(u_rows)
        inverse.append(m_rows)
        for i in soon:
            left[i] = left[i] - added([sides[i][j] * row_spread(u_rows, j) for j in range(ROWS)])
            right[i] = right[i] - added([sides[i][j] * row_spread(m_rows, j) for j in range(ROWS)])
        if k + 1 + AHEAD >= count:
            continue
        both = jnp.concatenate([u_rows, m_rows], axis=1)
        high = both.astype(jnp.bfloat16).astype(jnp.float32)
        low = both - high
        lhs = jnp.concatenate([high[:, :TILE], high[:, :TILE], low[:, :TILE], pad1], axis=0)
        rhs = jnp.concatenate([high, low, high, pad2], axis=0)
        update = lax.dot_general(
            lhs.astype(jnp.bfloat16),
            rhs.astype(jnp.bfloat16),
            TN,
            preferred_element_type=jnp.float32,
        )
        for i in range(k + 1 + AHEAD, count):
            rows = slice(ROWS * i, ROWS * (i + 1))
            left[i] = left[i] - update[rows, :TILE]
            right[i] = right[i] - update[rows, TILE:]
    return jnp.concatenate(upper, axis=0), jnp.concatenate(inverse, axis=0)


def leaf_kernel(diag_ref, basis_ref, after1, out_ref, schur_ref, work, u_tile, m_tile):
    basis = split(basis_ref[...])
    half = split(dot3(split(diag_ref[...]), basis))
    redundant = [part[:, :REDUN] for part in basis]
    skeleton = [part[:, REDUN:] for part in basis]
    top = dot3(redundant, half, TN)
    square = top[:, :REDUN]
    work[:, :REDUN] = 0.5 * (square + square.T)
    work[:, REDUN:] = top[:, REDUN:]
    schur_ref[...] = dot3(skeleton, [part[:, REDUN:] for part in half], TN)

    def step(k, carry):
        rows = pl.ds(pl.multiple_of(k * TILE, TILE), TILE)
        upper, inverse = tile_factor(work[rows, rows])
        u_tile[...] = upper
        m_tile[...] = inverse
        new_rows = dot3(split(m_tile[...]), split(work[rows, :]))
        work[rows, :] = new_rows
        work[rows, rows] = u_tile[...]

        @pl.when(k == 0)
        def _():
            parts = split(new_rows)
            side = [part[:, TILE:REDUN] for part in parts]
            work[TILE:, TILE:] = work[TILE:, TILE:] - dot3(side, [part[:, TILE:] for part in parts], TN)

        return carry

    lax.fori_loop(0, REDUN // TILE, step, 0)
    row = lax.broadcasted_iota(jnp.int32, (REDUN, REDUN), 0)
    col = lax.broadcasted_iota(jnp.int32, (REDUN, REDUN), 1)
    out_ref[:, :REDUN] = jnp.where(row <= col, work[:, :REDUN], 0.0).T
    coupled = work[:, REDUN:]
    out_ref[:, REDUN:] = coupled
    parts = split(coupled)
    schur_ref[...] = schur_ref[...] - dot3(parts, parts, TN)


def left_kernel(skel_ref, near_ref, after1, high_ref, low_ref, skel_high, skel_low):
    @pl.when(pl.program_id(0) == 0)
    def _():
        high, low = split(skel_ref[...].T)
        skel_high[...] = high
        skel_low[...] = low

    high, low = split(dot3((skel_high[...], skel_low[...]), split(near_ref[0])))
    high_ref[0] = high
    low_ref[0] = low


def source_of(leaf, near_ref, far_ref):
    slot = jnp.int32(0)
    for m in range(NEAR):
        slot = slot + jnp.where(near_ref[0, m] == leaf, m, 0)
    for f in range(FAR):
        slot = slot + jnp.where(far_ref[0, f] == leaf, NEAR + f, 0)
    return slot, jnp.minimum(slot, NEAR - 1), jnp.maximum(slot - NEAR, 0)


def sibling_slots(me_ref, near_ref, far_ref):
    return [source_of(jnp.bitwise_xor(me_ref[0], s), near_ref, far_ref) for s in range(1, GROUP)]


def sibling_kernel(me_ref, near_ref, far_ref, skel_ref, near_hbm, high_ref, low_ref, held, sems):
    slots = sibling_slots(me_ref, near_ref, far_ref)
    copies = [
        pltpu.make_async_copy(near_hbm.at[m], held.at[s], sems.at[s])
        for s, (_, m, _) in enumerate(slots)
    ]
    for copy in copies:
        copy.start()
    skel = split(skel_ref[...].T)
    for s in range(GROUP - 1):
        copies[s].wait()

        @pl.when(slots[s][0] < NEAR)
        def _(s=s):
            high, low = split(dot3(skel, split(held[s])))
            high_ref[s] = high
            low_ref[s] = low


def block_rows(s):
    return slice(s * RANK, (s + 1) * RANK)


def own_kernel(
    me_ref, near_ref, far_ref, high_hbm, low_hbm, far_hbm, schur_hbm, s1, s2, s3,
    out_ref, high_held, low_held, skel_held, sems, own_sem,
):
    slots = sibling_slots(me_ref, near_ref, far_ref)
    own_copy = pltpu.make_async_copy(schur_hbm, out_ref.at[block_rows(0), :], own_sem)
    near_copies = []
    far_copies = []
    for s, sibling in enumerate((s1, s2, s3)):
        near_copies.append(
            [
                pltpu.make_async_copy(high_hbm.at[s], high_held.at[s], sems.at[0, s]),
                pltpu.make_async_copy(low_hbm.at[s], low_held.at[s], sems.at[1, s]),
                pltpu.make_async_copy(sibling, skel_held.at[s], sems.at[2, s]),
            ]
        )
        far_copies.append(
            pltpu.make_async_copy(
                far_hbm.at[slots[s][2]], out_ref.at[block_rows(s + 1), :], sems.at[0, s]
            )
        )

        @pl.when(slots[s][0] < NEAR)
        def _(s=s):
            for copy in near_copies[s]:
                copy.start()

        @pl.when(slots[s][0] >= NEAR)
        def _(s=s):
            far_copies[s].start()

    own_copy.start()
    out_ref[GROUP * RANK :, :] = jnp.zeros((ROWS, RANK), jnp.float32)
    for s in range(GROUP - 1):

        @pl.when(slots[s][0] < NEAR)
        def _(s=s):
            for copy in near_copies[s]:
                copy.wait()
            out_ref[block_rows(s + 1), :] = dot3((high_held[s], low_held[s]), split(skel_held[s]))

        @pl.when(slots[s][0] >= NEAR)
        def _(s=s):
            far_copies[s].wait()

    own_copy.wait()


def side_kernel(blocks, members, me_ref, near_ref, far_ref, high_hbm, low_hbm, far_hbm, *rest):
    count = len(members)
    zs, (earlier, out_ref, z_held, high_held, low_held, far_held, h_high, h_low, s_high, s_low, sems) = (
        rest[: 2 * count],
        rest[2 * count :],
    )
    slots = []
    z_copies = []
    near_copies = []
    far_copies = []
    for side, shift in enumerate((blocks - GROUP, GROUP)):
        for place, s in enumerate(members):
            n = side * count + place
            leaf = lax.rem(jnp.bitwise_xor(me_ref[0], s) + shift, blocks)
            slot, m, f = source_of(leaf, near_ref, far_ref)
            slots.append(slot)
            z_copies.append(pltpu.make_async_copy(zs[n], z_held.at[n], sems.at[0, n]))
            near_copies.append(
                [
                    pltpu.make_async_copy(high_hbm.at[m], high_held.at[n], sems.at[1, n]),
                    pltpu.make_async_copy(low_hbm.at[m], low_held.at[n], sems.at[2, n]),
                ]
            )
            far_copies.append(pltpu.make_async_copy(far_hbm.at[f], far_held.at[n], sems.at[1, n]))
    for n in range(2 * count):
        z_copies[n].start()

        @pl.when(slots[n] < NEAR)
        def _(n=n):
            for copy in near_copies[n]:
                copy.start()

        @pl.when(slots[n] >= NEAR)
        def _(n=n):
            far_copies[n].start()

    for side in range(2):
        for place in range(count):
            n = side * count + place
            cols = slice(place * RANK, (place + 1) * RANK)
            z_copies[n].wait()

            @pl.when(slots[n] < NEAR)
            def _(n=n, cols=cols):
                for copy in near_copies[n]:
                    copy.wait()
                high, low = split(dot3((high_held[n], low_held[n]), split(z_held[n, :LEAF, :])))
                h_high[:, cols] = high
                h_low[:, cols] = low

            @pl.when(slots[n] >= NEAR)
            def _(n=n, cols=cols):
                far_copies[n].wait()
                high, low = split(far_held[n])
                h_high[:, cols] = high
                h_low[:, cols] = low

            high, low = split(z_held[n, LEAF:, :])
            s_high[cols, :] = high
            s_low[cols, :] = low
        half = slice(side * RANK, (side + 1) * RANK)
        total = dot3((h_high[...], h_low[...]), (s_high[...], s_low[...]))
        out_ref[:, half] = total


def partial_sums(p_high, p_low, h_refs, first, v_high, v_low):
    for s in range(2):
        line = [h_refs[s][block_rows((first + s) ^ t), :] for t in range(GROUP)]
        line = split(jnp.concatenate(line, axis=1))
        high, low = split(dot3(line, (p_high[...], p_low[...])))
        rows = slice(s * RANK, (s + 1) * RANK)
        v_high[rows, :] = high
        v_low[rows, :] = low


def load_bases(p_hbm, p_held, p_high, p_low, sems):
    copies = []
    for s, base in enumerate(p_hbm):
        rows = block_rows(s)
        copies.append(pltpu.make_async_copy(base, p_held.at[rows, :], sems.at[s]))
        copies[s].start()

    def finish(use=None):
        for s in range(GROUP):
            rows = block_rows(s)
            copies[s].wait()
            high, low = split(p_held[rows, :])
            p_high[rows, :] = high
            p_low[rows, :] = low
            if use is not None:
                use(rows)

    return finish


def chip_kernel(
    me_ref, h0, h1, p0, p1, p2, p3, after1, t_high, t_low, part_hbm,
    h_held, p_held, p_high, p_low, v_high, v_low, part, sems, p_sems, o_sems,
):
    member = lax.rem(me_ref[0], GROUP)
    slab = pl.ds(pl.multiple_of(member * RANK, RANK), RANK)
    finish = load_bases((p0, p1, p2, p3), p_held, p_high, p_low, p_sems)
    copies = [pltpu.make_async_copy(h, h_held.at[s], sems.at[s]) for s, h in enumerate((h0, h1))]
    for copy in copies:
        copy.start()

    def own_slab(rows):
        high, low = split(p_held[rows, slab].T)
        t_high[:, rows] = high
        t_low[:, rows] = low

    finish(own_slab)
    for copy in copies:
        copy.wait()
    partial_sums(p_high, p_low, h_held, 0, v_high, v_low)
    half = slice(0, 2 * RANK)
    sent = []
    for m in range(GROUP):
        cols = block_rows(m)
        part[cols, :] = dot3((p_high[half, cols], p_low[half, cols]), (v_high[...], v_low[...]), TN)
        sent.append(pltpu.make_async_copy(part.at[cols, :], part_hbm.at[cols, :], o_sems.at[m]))
        sent[m].start()
    for copy in sent:
        copy.wait()


def eliminate(work, u_tile, m_tile, first, last, before_last=None):
    def step(k, carry):
        if before_last is not None:
            pl.when(k == last - 1)(before_last)
        rows = pl.ds(pl.multiple_of(k * TILE, TILE), TILE)
        upper, inverse = tile_factor(work[rows, rows])
        u_tile[...] = upper
        m_tile[...] = inverse
        new_rows = dot3(split(m_tile[...]), split(work[rows, :]))
        work[rows, :] = new_rows
        work[rows, rows] = u_tile[...]
        parts = split(new_rows)
        for i in range(first + 1, PRED // TILE):

            @pl.when(i > k)
            def _(i=i):
                below = slice(i * TILE, (i + 1) * TILE)
                side = [part[:, below] for part in parts]
                right = [part[:, i * TILE :] for part in parts]
                work[below, i * TILE :] = work[below, i * TILE :] - dot3(side, right, TN)

        return carry

    lax.fori_loop(first, last, step, 0)


def parent_kernel(
    me_ref, h2, h3, p0, p1, p2, p3, part_hbm, work_hbm, edge_ref,
    h_held, p_held, p_high, p_low, v_high, v_low, part, whole, work, u_tile, m_tile, sems, p_sems, o_sems,
):
    member = lax.rem(me_ref[0], GROUP)
    copies = [pltpu.make_async_copy(h, h_held.at[s], sems.at[s]) for s, h in enumerate((h2, h3))]
    for copy in copies:
        copy.start()
    finish = load_bases((p0, p1, p2, p3), p_held, p_high, p_low, p_sems)
    part_copy = pltpu.make_async_copy(part_hbm, part, sems.at[2])
    part_copy.start()
    finish()
    for copy in copies:
        copy.wait()
    partial_sums(p_high, p_low, h_held, 2, v_high, v_low)
    half = slice(2 * RANK, PAR)
    part_copy.wait()
    for m in range(GROUP):
        cols = block_rows(m)
        whole[cols, :] = part[cols, :] + dot3(
            (p_high[half, cols], p_low[half, cols]), (v_high[...], v_low[...]), TN
        )
    square = whole[:PRED, :PRED]
    work[:, :PRED] = 0.5 * (square + square.T)
    work[:, PRED:PAR] = whole[:PRED, PRED:]
    work[:, PAR:] = whole[PRED:, :PRED].T
    slab = pl.ds(pl.multiple_of(member * RANK, RANK), RANK)
    edge_ref[...] = whole[slab, PRED:]
    done = (EARLY - 1) * TILE
    held_rows = pltpu.make_async_copy(work.at[:done, :], work_hbm.at[:done, :], o_sems.at[0])
    open_rows = pltpu.make_async_copy(work.at[done:, :], work_hbm.at[done:, :], o_sems.at[1])
    eliminate(work, u_tile, m_tile, 0, EARLY, held_rows.start)
    open_rows.start()
    held_rows.wait()
    open_rows.wait()


def finish_kernel(me_ref, work_hbm, edge_in, after1, factor_ref, edge_ref, work, u_tile, m_tile, sems):
    member = lax.rem(me_ref[0], GROUP)
    done = EARLY * TILE
    open_rows = pltpu.make_async_copy(work_hbm.at[done:, :], work.at[done:, :], sems.at[0])
    held_rows = pltpu.make_async_copy(work_hbm.at[:done, :], work.at[:done, :], sems.at[1])
    open_rows.start()
    held_rows.start()
    open_rows.wait()
    eliminate(work, u_tile, m_tile, EARLY, PRED // TILE)
    held_rows.wait()
    row = lax.broadcasted_iota(jnp.int32, (PRED, RANK), 0)
    col = lax.broadcasted_iota(jnp.int32, (PRED, RANK), 1) + member * RANK
    slab = pl.ds(pl.multiple_of(member * RANK, RANK), RANK)
    factor_ref[...] = jnp.where(row <= col, work[:, slab], 0.0).T
    edge_ref[...] = edge_in[...]

    @pl.when(member == GROUP - 1)
    def _():
        product = dot3(split(work[:, PAR:]), split(work[:, PRED:PAR]), TN)
        edge_ref[...] = edge_in[...] - product


def couple_kernel(t_high, t_low, v0, v1, v2, v3, edge_ref, out_ref):
    total = jnp.zeros((RANK, 2 * RANK), jnp.float32)
    for s, v_ref in enumerate((v0, v1, v2, v3)):
        cols = block_rows(s)
        total = total + dot3((t_high[:, cols], t_low[:, cols]), split(v_ref[...]))
    out_ref[:, :RANK] = total[:, :RANK]
    out_ref[:, RANK : 2 * RANK] = edge_ref[...]
    out_ref[:, 2 * RANK :] = total[:, RANK:]


def swapped(value, axis, mask):
    pairs = [(source, source ^ mask) for source in range(lax.axis_size(axis))]
    return lax.ppermute(value, axis, pairs)


def shifted(value, axis, steps):
    count = lax.axis_size(axis)
    pairs = [(source, (source + steps) % count) for source in range(count)]
    return lax.ppermute(value, axis, pairs)


def after(value, *earlier):
    return lax.optimization_barrier((value, *earlier))[0]


def gathered(value, axis, *earlier):
    core = swapped(value, axis, 1)
    chip = swapped(value, axis, 2)
    both = swapped(after(chip, *earlier), axis, 1)
    return [value, core, chip, both]


def call(kernel, name, ins, outs, scratch, *operands, flops=1, spaces=None, limit=VMEM_BYTES):
    return pl.pallas_call(
        kernel,
        in_specs=ins,
        out_specs=spaces or [in_vmem()] * len(outs),
        out_shape=[jax.ShapeDtypeStruct(shape, dtype) for shape, dtype in outs],
        scratch_shapes=scratch,
        compiler_params=params(limit),
        cost_estimate=pl.CostEstimate(flops=flops, bytes_accessed=1, transcendentals=0),

        name=name,
    )(*operands)


def anywhere():
    return pl.BlockSpec(memory_space=pl.ANY)


def on_device(
    diag_block, near_blocks, far_coupling, leaf_basis, parent_basis, near_index, far_index
):
    blocks = lax.axis_size("blk")
    me = lax.axis_index("blk").astype(jnp.int32).reshape(1)
    basis = leaf_basis[0]
    skeleton = basis[:, REDUN:]
    near = near_blocks[0]
    far = far_coupling[0]
    f32, b16 = jnp.float32, jnp.bfloat16

    load = jnp.concatenate([skeleton, parent_basis[:, PRED:]], axis=0)
    prev_load = shifted(load, "blk", GROUP)
    next_load = shifted(load, "blk", -GROUP)

    base_chip = swapped(parent_basis, "blk", 2)

    sib_high, sib_low = call(
        sibling_kernel,
        "sibling_products",
        [in_smem()] * 3 + [in_vmem(), anywhere()],
        [((GROUP - 1, RANK, LEAF), b16)] * 2,
        [pltpu.VMEM((GROUP - 1, LEAF, LEAF), f32), pltpu.SemaphoreType.DMA((GROUP - 1,))],
        me,
        near_index,
        far_index,
        skeleton,
        near,
        limit=VMEM_EARLY,
    )
    leaf_out, leaf_schur = call(
        leaf_kernel,
        "leaf_factor",
        [in_vmem()] * 2 + [anywhere()],
        [((REDUN, LEAF), f32), ((RANK, RANK), f32)],
        [pltpu.VMEM((REDUN, LEAF), f32), pltpu.VMEM((TILE, TILE), f32), pltpu.VMEM((TILE, TILE), f32)],
        diag_block[0],
        basis,
        sib_high,
        flops=MIDDLE,
        limit=VMEM_EARLY,
    )
    skel_chip = swapped(skeleton, "blk", 2)
    skel_core = swapped(skeleton, "blk", 1)
    skels = [skeleton, skel_core, skel_chip, swapped(skel_chip, "blk", 1)]
    (own,) = call(
        own_kernel,
        "own_window",
        [in_smem()] * 3 + [anywhere()] * 7,
        [((GROUP * RANK + ROWS, RANK), f32)],
        [pltpu.VMEM((GROUP - 1, RANK, LEAF), b16)] * 2
        + [
            pltpu.VMEM((GROUP - 1, LEAF, RANK), f32),
            pltpu.SemaphoreType.DMA((3, GROUP - 1)),
            pltpu.SemaphoreType.DMA,
        ],
        me,
        near_index,
        far_index,
        sib_high,
        sib_low,
        far,
        leaf_schur,
        *skels[1:],
    )
    own_core = swapped(own, "blk", 1)
    own_chip = swapped(own, "blk", 2)

    left_high, left_low = pl.pallas_call(
        left_kernel,
        grid=(NEAR,),
        in_specs=[
            pl.BlockSpec((LEAF, RANK), lambda m: (0, 1)),
            pl.BlockSpec((1, LEAF, LEAF), lambda m: (m, 0, 0)),
            anywhere(),
        ],
        out_specs=[pl.BlockSpec((1, RANK, LEAF), lambda m: (m, 0, 0))] * 2,
        out_shape=[jax.ShapeDtypeStruct((NEAR, RANK, LEAF), b16)] * 2,
        scratch_shapes=[pltpu.VMEM((RANK, LEAF), b16)] * 2,
        compiler_params=params(),
        cost_estimate=pl.CostEstimate(flops=1, bytes_accessed=1, transcendentals=0),

        name="left_products",
    )(basis, near, own)
    base_core = swapped(after(parent_basis, left_high), "blk", 1)
    base_both = swapped(after(base_chip, left_high, prev_load, next_load), "blk", 1)
    bases = [parent_basis, base_core, base_chip, base_both]
    dma = pltpu.SemaphoreType.DMA
    loads = [
        pltpu.VMEM((2, GROUP * RANK + ROWS, RANK), f32),
        pltpu.VMEM((PAR, PAR), f32),
        pltpu.VMEM((PAR, PAR), b16),
        pltpu.VMEM((PAR, PAR), b16),
        pltpu.VMEM((2 * RANK, PAR), b16),
        pltpu.VMEM((2 * RANK, PAR), b16),
        pltpu.VMEM((PAR, PAR), f32),
    ]
    t_high, t_low, part = call(
        chip_kernel,
        "chip_sums",
        [in_smem()] + [anywhere()] * 7,
        [((RANK, PAR), b16)] * 2 + [((PAR, PAR), f32)],
        loads + [dma((2,)), dma((GROUP,)), dma((GROUP,))],
        me,
        own,
        own_core,
        *bases,
        left_high,
        spaces=[in_vmem(), in_vmem(), anywhere()],
    )
    own_both = swapped(after(own_chip, part), "blk", 1)
    prev_load = after(prev_load, part)
    next_load = after(next_load, part)
    tiles = [pltpu.VMEM((TILE, TILE), f32)] * 2
    work, edge_rows = call(
        parent_kernel,
        "parent_factor",
        [in_smem()] + [anywhere()] * 7,
        [((PRED, WIDE), f32), ((RANK, RANK), f32)],
        loads
        + [pltpu.VMEM((PAR, PAR), f32), pltpu.VMEM((PRED, WIDE), f32)]
        + tiles
        + [dma((3,)), dma((GROUP,)), dma((2,))],
        me,
        own_chip,
        own_both,
        *bases,
        part,
        spaces=[anywhere(), in_vmem()],
    )
    from_prev = gathered(prev_load, "blk", edge_rows)
    from_next = gathered(next_load, "blk", edge_rows)

    def windows(members, name, earlier):
        count = len(members)
        return call(
            functools.partial(side_kernel, blocks, members),
            name,
            [in_smem()] * 3 + [anywhere()] * (4 + 2 * count),
            [((RANK, 2 * RANK), f32)],
            [
                pltpu.VMEM((2 * count, LEAF + RANK, RANK), f32),
                pltpu.VMEM((2 * count, RANK, LEAF), b16),
                pltpu.VMEM((2 * count, RANK, LEAF), b16),
                pltpu.VMEM((2 * count, RANK, RANK), f32),
                pltpu.VMEM((RANK, count * RANK), b16),
                pltpu.VMEM((RANK, count * RANK), b16),
                pltpu.VMEM((count * RANK, RANK), b16),
                pltpu.VMEM((count * RANK, RANK), b16),
                dma((3, 2 * count)),
            ],
            me,
            near_index,
            far_index,
            left_high,
            left_low,
            far,
            *[from_prev[s] for s in members],
            *[from_next[s] for s in members],
            earlier,
        )[0]

    side = windows((0, 1, 2, 3), "side_windows", edge_rows)
    factor_rows, edge_rows = call(
        finish_kernel,
        "parent_finish",
        [in_smem(), anywhere(), in_vmem(), anywhere()],
        [((RANK, PRED), f32), ((RANK, RANK), f32)],
        [pltpu.VMEM((PRED, WIDE), f32)] + tiles + [pltpu.SemaphoreType.DMA((2,))],
        me,
        work,
        edge_rows,
        side,
    )
    sides = gathered(side, "blk", edge_rows)
    (coupling_rows,) = call(
        couple_kernel,
        "coupling",
        [in_vmem()] * 7,
        [((RANK, 3 * RANK), f32)],
        [],
        t_high,
        t_low,
        *sides,
        edge_rows,
    )
    return (leaf_out, factor_rows, coupling_rows)


def solution(mesh):
    placed = (
        P("blk", None, None),
        P("blk", None, None, None),
        P("blk", None, None, None),
        P("blk", None, None),
        P("blk", None),
        P("blk", None),
        P("blk", None),
    )
    return jax.shard_map(
        on_device,
        mesh=mesh,
        in_specs=placed,
        out_specs=(P("blk", None), P("blk", None), P("blk", None)),
        check_vma=False,
    )
```

```python
import functools

import jax
import jax.numpy as jnp
from jax import lax
from jax.experimental import pallas as pl
from jax.experimental.pallas import tpu as pltpu
from jax.sharding import PartitionSpec as P

LEAF = 512
RANK = 256
NEAR = 6
GROUP = 4
REDUN = 256
PAR = 1024
PRED = 768
FAR = 5
TILE = 128
ROWS = 8
WIDE = PRED + 2 * RANK
EARLY = 4
AHEAD = 2
MIDDLE = 30_000_000_000

MIB = 1024 * 1024
VMEM_BYTES = 64 * MIB
VMEM_EARLY = 48 * MIB

NN = (((1,), (0,)), ((), ()))
TN = (((0,), (0,)), ((), ()))


def params(limit=VMEM_BYTES):
    return pltpu.CompilerParams(vmem_limit_bytes=limit)


def in_vmem():
    return pl.BlockSpec(memory_space=pltpu.VMEM)


def in_smem():
    return pl.BlockSpec(memory_space=pltpu.SMEM)


def split(value):
    high = value.astype(jnp.bfloat16)
    low = (value - high.astype(jnp.float32)).astype(jnp.bfloat16)
    return high, low


def dot3(left, right, dims=NN):
    def one(a, b):
        return lax.dot_general(a, b, dims, preferred_element_type=jnp.float32)

    return one(left[0], right[0]) + (one(left[0], right[1]) + one(left[1], right[0]))


def lane_spread(value, lane):
    return jnp.broadcast_to(value[:, lane : lane + 1], (ROWS, TILE))


def row_spread(value, row):
    return jnp.broadcast_to(value[row : row + 1, :], (ROWS, TILE))


def small_inverse(entry):
    entry = dict(entry)
    low = {}
    inv = {}
    for j in range(ROWS):
        root = lax.rsqrt(entry[j, j])
        for i in range(j + 1, ROWS):
            low[i, j] = entry[i, j] * root
        for k in range(j + 1, ROWS):
            for i in range(k, ROWS):
                entry[i, k] = entry[i, k] - low[i, j] * low[k, j]
        inv[j, j] = root
        for t in range(j):
            total = low[j, t] * inv[t, t]
            for k in range(t + 1, j):
                total = total + low[j, k] * inv[k, t]
            inv[j, t] = -(total * root)
    return inv


def weighted(inv, j, values):
    total = inv[j, 0] * values[0]
    for t in range(1, j + 1):
        total = total + inv[j, t] * values[t]
    return total


def added(terms):
    while len(terms) > 1:
        terms = [terms[i] + terms[i + 1] for i in range(0, len(terms), 2)]
    return terms[0]


def tile_factor(square):
    count = TILE // ROWS
    row = lax.broadcasted_iota(jnp.int32, (ROWS, TILE), 0)
    col = lax.broadcasted_iota(jnp.int32, (ROWS, TILE), 1)
    left = [square[ROWS * i : ROWS * (i + 1), :] for i in range(count)]
    right = [jnp.where(row + ROWS * i == col, 1.0, 0.0).astype(jnp.float32) for i in range(count)]
    upper = []
    inverse = []
    pad1 = jnp.zeros((ROWS, TILE), jnp.float32)
    pad2 = jnp.zeros((ROWS, 2 * TILE), jnp.float32)
    cols = [lane_spread(left[0], j) for j in range(ROWS)]
    for k in range(count):
        inv = small_inverse(
            {(i, j): row_spread(cols[j], i) for j in range(ROWS) for i in range(j, ROWS)}
        )
        soon = range(k + 1, min(k + 1 + AHEAD, count))
        sides = {}
        for i in soon:
            raw = [lane_spread(left[i], ROWS * k + t) for t in range(ROWS)]
            sides[i] = [weighted(inv, j, raw) for j in range(ROWS)]
        if k + 1 < count:
            side = sides[k + 1]
            cols = [
                lane_spread(left[k + 1], ROWS * (k + 1) + j)
                - added([side[t] * row_spread(side[t], j) for t in range(ROWS)])
                for j in range(ROWS)
            ]
        u_rows = m_rows = None
        for j in range(ROWS):
            weight = inv[ROWS - 1, j]
            for i in range(ROWS - 2, j - 1, -1):
                weight = jnp.where(row == i, inv[i, j], weight)
            if j > 0:
                weight = jnp.where(row >= j, weight, 0.0)
            u_term = weight * row_spread(left[k], j)
            m_term = weight * row_spread(right[k], j)
            u_rows = u_term if u_rows is None else u_rows + u_term
            m_rows = m_term if m_rows is None else m_rows + m_term
        u_rows = jnp.where(col >= row + ROWS * k, u_rows, 0.0)
        upper.append(u_rows)
        inverse.append(m_rows)
        for i in soon:
            left[i] = left[i] - added([sides[i][j] * row_spread(u_rows, j) for j in range(ROWS)])
            right[i] = right[i] - added([sides[i][j] * row_spread(m_rows, j) for j in range(ROWS)])
        if k + 1 + AHEAD >= count:
            continue
        both = jnp.concatenate([u_rows, m_rows], axis=1)
        high = both.astype(jnp.bfloat16).astype(jnp.float32)
        low = both - high
        lhs = jnp.concatenate([high[:, :TILE], high[:, :TILE], low[:, :TILE], pad1], axis=0)
        rhs = jnp.concatenate([high, low, high, pad2], axis=0)
        update = lax.dot_general(
            lhs.astype(jnp.bfloat16),
            rhs.astype(jnp.bfloat16),
            TN,
            preferred_element_type=jnp.float32,
        )
        for i in range(k + 1 + AHEAD, count):
            rows = slice(ROWS * i, ROWS * (i + 1))
            left[i] = left[i] - update[rows, :TILE]
            right[i] = right[i] - update[rows, TILE:]
    return jnp.concatenate(upper, axis=0), jnp.concatenate(inverse, axis=0)


def leaf_kernel(diag_ref, basis_ref, after1, out_ref, schur_ref, work, u_tile, m_tile):
    basis = split(basis_ref[...])
    half = split(dot3(split(diag_ref[...]), basis))
    redundant = [part[:, :REDUN] for part in basis]
    skeleton = [part[:, REDUN:] for part in basis]
    top = dot3(redundant, half, TN)
    square = top[:, :REDUN]
    work[:, :REDUN] = 0.5 * (square + square.T)
    work[:, REDUN:] = top[:, REDUN:]
    schur_ref[...] = dot3(skeleton, [part[:, REDUN:] for part in half], TN)

    def step(k, carry):
        rows = pl.ds(pl.multiple_of(k * TILE, TILE), TILE)
        upper, inverse = tile_factor(work[rows, rows])
        u_tile[...] = upper
        m_tile[...] = inverse
        new_rows = dot3(split(m_tile[...]), split(work[rows, :]))
        work[rows, :] = new_rows
        work[rows, rows] = u_tile[...]

        @pl.when(k == 0)
        def _():
            parts = split(new_rows)
            side = [part[:, TILE:REDUN] for part in parts]
            work[TILE:, TILE:] = work[TILE:, TILE:] - dot3(side, [part[:, TILE:] for part in parts], TN)

        return carry

    lax.fori_loop(0, REDUN // TILE, step, 0)
    row = lax.broadcasted_iota(jnp.int32, (REDUN, REDUN), 0)
    col = lax.broadcasted_iota(jnp.int32, (REDUN, REDUN), 1)
    out_ref[:, :REDUN] = jnp.where(row <= col, work[:, :REDUN], 0.0).T
    coupled = work[:, REDUN:]
    out_ref[:, REDUN:] = coupled
    parts = split(coupled)
    schur_ref[...] = schur_ref[...] - dot3(parts, parts, TN)


def left_kernel(skel_ref, near_ref, after1, high_ref, low_ref, skel_high, skel_low):
    @pl.when(pl.program_id(0) == 0)
    def _():
        high, low = split(skel_ref[...].T)
        skel_high[...] = high
        skel_low[...] = low

    high, low = split(dot3((skel_high[...], skel_low[...]), split(near_ref[0])))
    high_ref[0] = high
    low_ref[0] = low


def source_of(leaf, near_ref, far_ref):
    slot = jnp.int32(0)
    for m in range(NEAR):
        slot = slot + jnp.where(near_ref[0, m] == leaf, m, 0)
    for f in range(FAR):
        slot = slot + jnp.where(far_ref[0, f] == leaf, NEAR + f, 0)
    return slot, jnp.minimum(slot, NEAR - 1), jnp.maximum(slot - NEAR, 0)


def sibling_slots(me_ref, near_ref, far_ref):
    return [source_of(jnp.bitwise_xor(me_ref[0], s), near_ref, far_ref) for s in range(1, GROUP)]


def sibling_kernel(me_ref, near_ref, far_ref, skel_ref, near_hbm, high_ref, low_ref, held, sems):
    slots = sibling_slots(me_ref, near_ref, far_ref)
    copies = [
        pltpu.make_async_copy(near_hbm.at[m], held.at[s], sems.at[s])
        for s, (_, m, _) in enumerate(slots)
    ]
    for copy in copies:
        copy.start()
    skel = split(skel_ref[...].T)
    for s in range(GROUP - 1):
        copies[s].wait()

        @pl.when(slots[s][0] < NEAR)
        def _(s=s):
            high, low = split(dot3(skel, split(held[s])))
            high_ref[s] = high
            low_ref[s] = low


def block_rows(s):
    return slice(s * RANK, (s + 1) * RANK)


def own_kernel(
    me_ref, near_ref, far_ref, high_hbm, low_hbm, far_hbm, schur_hbm, s1, s2, s3,
    out_ref, high_held, low_held, skel_held, sems, own_sem,
):
    slots = sibling_slots(me_ref, near_ref, far_ref)
    own_copy = pltpu.make_async_copy(schur_hbm, out_ref.at[block_rows(0), :], own_sem)
    near_copies = []
    far_copies = []
    for s, sibling in enumerate((s1, s2, s3)):
        near_copies.append(
            [
                pltpu.make_async_copy(high_hbm.at[s], high_held.at[s], sems.at[0, s]),
                pltpu.make_async_copy(low_hbm.at[s], low_held.at[s], sems.at[1, s]),
                pltpu.make_async_copy(sibling, skel_held.at[s], sems.at[2, s]),
            ]
        )
        far_copies.append(
            pltpu.make_async_copy(
                far_hbm.at[slots[s][2]], out_ref.at[block_rows(s + 1), :], sems.at[0, s]
            )
        )

        @pl.when(slots[s][0] < NEAR)
        def _(s=s):
            for copy in near_copies[s]:
                copy.start()

        @pl.when(slots[s][0] >= NEAR)
        def _(s=s):
            far_copies[s].start()

    own_copy.start()
    out_ref[GROUP * RANK :, :] = jnp.zeros((ROWS, RANK), jnp.float32)
    for s in range(GROUP - 1):

        @pl.when(slots[s][0] < NEAR)
        def _(s=s):
            for copy in near_copies[s]:
                copy.wait()
            out_ref[block_rows(s + 1), :] = dot3((high_held[s], low_held[s]), split(skel_held[s]))

        @pl.when(slots[s][0] >= NEAR)
        def _(s=s):
            far_copies[s].wait()

    own_copy.wait()


def side_kernel(blocks, members, me_ref, near_ref, far_ref, high_hbm, low_hbm, far_hbm, *rest):
    count = len(members)
    zs, (earlier, out_ref, z_held, high_held, low_held, far_held, h_high, h_low, s_high, s_low, sems) = (
        rest[: 2 * count],
        rest[2 * count :],
    )
    slots = []
    z_copies = []
    near_copies = []
    far_copies = []
    for side, shift in enumerate((blocks - GROUP, GROUP)):
        for place, s in enumerate(members):
            n = side * count + place
            leaf = lax.rem(jnp.bitwise_xor(me_ref[0], s) + shift, blocks)
            slot, m, f = source_of(leaf, near_ref, far_ref)
            slots.append(slot)
            z_copies.append(pltpu.make_async_copy(zs[n], z_held.at[n], sems.at[0, n]))
            near_copies.append(
                [
                    pltpu.make_async_copy(high_hbm.at[m], high_held.at[n], sems.at[1, n]),
                    pltpu.make_async_copy(low_hbm.at[m], low_held.at[n], sems.at[2, n]),
                ]
            )
            far_copies.append(pltpu.make_async_copy(far_hbm.at[f], far_held.at[n], sems.at[1, n]))
    for n in range(2 * count):
        z_copies[n].start()

        @pl.when(slots[n] < NEAR)
        def _(n=n):
            for copy in near_copies[n]:
                copy.start()

        @pl.when(slots[n] >= NEAR)
        def _(n=n):
            far_copies[n].start()

    for side in range(2):
        for place in range(count):
            n = side * count + place
            cols = slice(place * RANK, (place + 1) * RANK)
            z_copies[n].wait()

            @pl.when(slots[n] < NEAR)
            def _(n=n, cols=cols):
                for copy in near_copies[n]:
                    copy.wait()
                high, low = split(dot3((high_held[n], low_held[n]), split(z_held[n, :LEAF, :])))
                h_high[:, cols] = high
                h_low[:, cols] = low

            @pl.when(slots[n] >= NEAR)
            def _(n=n, cols=cols):
                far_copies[n].wait()
                high, low = split(far_held[n])
                h_high[:, cols] = high
                h_low[:, cols] = low

            high, low = split(z_held[n, LEAF:, :])
            s_high[cols, :] = high
            s_low[cols, :] = low
        half = slice(side * RANK, (side + 1) * RANK)
        total = dot3((h_high[...], h_low[...]), (s_high[...], s_low[...]))
        out_ref[:, half] = total


def partial_sums(p_high, p_low, h_refs, first, v_high, v_low):
    for s in range(2):
        line = [h_refs[s][block_rows((first + s) ^ t), :] for t in range(GROUP)]
        line = split(jnp.concatenate(line, axis=1))
        high, low = split(dot3(line, (p_high[...], p_low[...])))
        rows = slice(s * RANK, (s + 1) * RANK)
        v_high[rows, :] = high
        v_low[rows, :] = low


def load_bases(p_hbm, p_held, p_high, p_low, sems):
    copies = []
    for s, base in enumerate(p_hbm):
        rows = block_rows(s)
        copies.append(pltpu.make_async_copy(base, p_held.at[rows, :], sems.at[s]))
        copies[s].start()

    def finish(use=None):
        for s in range(GROUP):
            rows = block_rows(s)
            copies[s].wait()
            high, low = split(p_held[rows, :])
            p_high[rows, :] = high
            p_low[rows, :] = low
            if use is not None:
                use(rows)

    return finish


def chip_kernel(
    me_ref, h0, h1, p0, p1, p2, p3, after1, t_high, t_low, part_hbm,
    h_held, p_held, p_high, p_low, v_high, v_low, part, sems, p_sems, o_sems,
):
    member = lax.rem(me_ref[0], GROUP)
    slab = pl.ds(pl.multiple_of(member * RANK, RANK), RANK)
    finish = load_bases((p0, p1, p2, p3), p_held, p_high, p_low, p_sems)
    copies = [pltpu.make_async_copy(h, h_held.at[s], sems.at[s]) for s, h in enumerate((h0, h1))]
    for copy in copies:
        copy.start()

    def own_slab(rows):
        high, low = split(p_held[rows, slab].T)
        t_high[:, rows] = high
        t_low[:, rows] = low

    finish(own_slab)
    for copy in copies:
        copy.wait()
    partial_sums(p_high, p_low, h_held, 0, v_high, v_low)
    half = slice(0, 2 * RANK)
    sent = []
    for m in range(GROUP):
        cols = block_rows(m)
        part[cols, :] = dot3((p_high[half, cols], p_low[half, cols]), (v_high[...], v_low[...]), TN)
        sent.append(pltpu.make_async_copy(part.at[cols, :], part_hbm.at[cols, :], o_sems.at[m]))
        sent[m].start()
    for copy in sent:
        copy.wait()


def eliminate(work, u_tile, m_tile, first, last, before_last=None):
    def step(k, carry):
        if before_last is not None:
            pl.when(k == last - 1)(before_last)
        rows = pl.ds(pl.multiple_of(k * TILE, TILE), TILE)
        upper, inverse = tile_factor(work[rows, rows])
        u_tile[...] = upper
        m_tile[...] = inverse
        new_rows = dot3(split(m_tile[...]), split(work[rows, :]))
        work[rows, :] = new_rows
        work[rows, rows] = u_tile[...]
        parts = split(new_rows)
        for i in range(first + 1, PRED // TILE):

            @pl.when(i > k)
            def _(i=i):
                below = slice(i * TILE, (i + 1) * TILE)
                side = [part[:, below] for part in parts]
                right = [part[:, i * TILE :] for part in parts]
                work[below, i * TILE :] = work[below, i * TILE :] - dot3(side, right, TN)

        return carry

    lax.fori_loop(first, last, step, 0)


def parent_kernel(
    me_ref, h2, h3, p0, p1, p2, p3, part_hbm, work_hbm, edge_ref,
    h_held, p_held, p_high, p_low, v_high, v_low, part, whole, work, u_tile, m_tile, sems, p_sems, o_sems,
):
    member = lax.rem(me_ref[0], GROUP)
    copies = [pltpu.make_async_copy(h, h_held.at[s], sems.at[s]) for s, h in enumerate((h2, h3))]
    for copy in copies:
        copy.start()
    finish = load_bases((p0, p1, p2, p3), p_held, p_high, p_low, p_sems)
    part_copy = pltpu.make_async_copy(part_hbm, part, sems.at[2])
    part_copy.start()
    finish()
    for copy in copies:
        copy.wait()
    partial_sums(p_high, p_low, h_held, 2, v_high, v_low)
    half = slice(2 * RANK, PAR)
    part_copy.wait()
    for m in range(GROUP):
        cols = block_rows(m)
        whole[cols, :] = part[cols, :] + dot3(
            (p_high[half, cols], p_low[half, cols]), (v_high[...], v_low[...]), TN
        )
    square = whole[:PRED, :PRED]
    work[:, :PRED] = 0.5 * (square + square.T)
    work[:, PRED:PAR] = whole[:PRED, PRED:]
    work[:, PAR:] = whole[PRED:, :PRED].T
    slab = pl.ds(pl.multiple_of(member * RANK, RANK), RANK)
    edge_ref[...] = whole[slab, PRED:]
    done = (EARLY - 1) * TILE
    held_rows = pltpu.make_async_copy(work.at[:done, :], work_hbm.at[:done, :], o_sems.at[0])
    open_rows = pltpu.make_async_copy(work.at[done:, :], work_hbm.at[done:, :], o_sems.at[1])
    eliminate(work, u_tile, m_tile, 0, EARLY, held_rows.start)
    open_rows.start()
    held_rows.wait()
    open_rows.wait()


def finish_kernel(me_ref, work_hbm, edge_in, after1, factor_ref, edge_ref, work, u_tile, m_tile, sems):
    member = lax.rem(me_ref[0], GROUP)
    done = EARLY * TILE
    open_rows = pltpu.make_async_copy(work_hbm.at[done:, :], work.at[done:, :], sems.at[0])
    held_rows = pltpu.make_async_copy(work_hbm.at[:done, :], work.at[:done, :], sems.at[1])
    open_rows.start()
    held_rows.start()
    open_rows.wait()
    eliminate(work, u_tile, m_tile, EARLY, PRED // TILE)
    held_rows.wait()
    row = lax.broadcasted_iota(jnp.int32, (PRED, RANK), 0)
    col = lax.broadcasted_iota(jnp.int32, (PRED, RANK), 1) + member * RANK
    slab = pl.ds(pl.multiple_of(member * RANK, RANK), RANK)
    factor_ref[...] = jnp.where(row <= col, work[:, slab], 0.0).T
    edge_ref[...] = edge_in[...]

    @pl.when(member == GROUP - 1)
    def _():
        product = dot3(split(work[:, PAR:]), split(work[:, PRED:PAR]), TN)
        edge_ref[...] = edge_in[...] - product


def couple_kernel(t_high, t_low, v0, v1, v2, v3, edge_ref, out_ref):
    total = jnp.zeros((RANK, 2 * RANK), jnp.float32)
    for s, v_ref in enumerate((v0, v1, v2, v3)):
        cols = block_rows(s)
        total = total + dot3((t_high[:, cols], t_low[:, cols]), split(v_ref[...]))
    out_ref[:, :RANK] = total[:, :RANK]
    out_ref[:, RANK : 2 * RANK] = edge_ref[...]
    out_ref[:, 2 * RANK :] = total[:, RANK:]


def swapped(value, axis, mask):
    pairs = [(source, source ^ mask) for source in range(lax.axis_size(axis))]
    return lax.ppermute(value, axis, pairs)


def shifted(value, axis, steps):
    count = lax.axis_size(axis)
    pairs = [(source, (source + steps) % count) for source in range(count)]
    return lax.ppermute(value, axis, pairs)


def after(value, *earlier):
    return lax.optimization_barrier((value, *earlier))[0]


def gathered(value, axis, *earlier):
    core = swapped(value, axis, 1)
    chip = swapped(value, axis, 2)
    both = swapped(after(chip, *earlier), axis, 1)
    return [value, core, chip, both]


def call(kernel, name, ins, outs, scratch, *operands, flops=1, spaces=None, limit=VMEM_BYTES):
    return pl.pallas_call(
        kernel,
        in_specs=ins,
        out_specs=spaces or [in_vmem()] * len(outs),
        out_shape=[jax.ShapeDtypeStruct(shape, dtype) for shape, dtype in outs],
        scratch_shapes=scratch,
        compiler_params=params(limit),
        cost_estimate=pl.CostEstimate(flops=flops, bytes_accessed=1, transcendentals=0),

        name=name,
    )(*operands)


def anywhere():
    return pl.BlockSpec(memory_space=pl.ANY)


def on_device(
    diag_block, near_blocks, far_coupling, leaf_basis, parent_basis, near_index, far_index
):
    blocks = lax.axis_size("blk")
    me = lax.axis_index("blk").astype(jnp.int32).reshape(1)
    basis = leaf_basis[0]
    skeleton = basis[:, REDUN:]
    near = near_blocks[0]
    far = far_coupling[0]
    f32, b16 = jnp.float32, jnp.bfloat16

    load = jnp.concatenate([skeleton, parent_basis[:, PRED:]], axis=0)
    prev_load = shifted(load, "blk", GROUP)
    next_load = shifted(load, "blk", -GROUP)

    base_chip = swapped(parent_basis, "blk", 2)

    sib_high, sib_low = call(
        sibling_kernel,
        "sibling_products",
        [in_smem()] * 3 + [in_vmem(), anywhere()],
        [((GROUP - 1, RANK, LEAF), b16)] * 2,
        [pltpu.VMEM((GROUP - 1, LEAF, LEAF), f32), pltpu.SemaphoreType.DMA((GROUP - 1,))],
        me,
        near_index,
        far_index,
        skeleton,
        near,
        limit=VMEM_EARLY,
    )
    leaf_out, leaf_schur = call(
        leaf_kernel,
        "leaf_factor",
        [in_vmem()] * 2 + [anywhere()],
        [((REDUN, LEAF), f32), ((RANK, RANK), f32)],
        [pltpu.VMEM((REDUN, LEAF), f32), pltpu.VMEM((TILE, TILE), f32), pltpu.VMEM((TILE, TILE), f32)],
        diag_block[0],
        basis,
        sib_high,
        flops=MIDDLE,
        limit=VMEM_EARLY,
    )
    skel_chip = swapped(skeleton, "blk", 2)
    skel_core = swapped(skeleton, "blk", 1)
    skels = [skeleton, skel_core, skel_chip, swapped(skel_chip, "blk", 1)]
    (own,) = call(
        own_kernel,
        "own_window",
        [in_smem()] * 3 + [anywhere()] * 7,
        [((GROUP * RANK + ROWS, RANK), f32)],
        [pltpu.VMEM((GROUP - 1, RANK, LEAF), b16)] * 2
        + [
            pltpu.VMEM((GROUP - 1, LEAF, RANK), f32),
            pltpu.SemaphoreType.DMA((3, GROUP - 1)),
            pltpu.SemaphoreType.DMA,
        ],
        me,
        near_index,
        far_index,
        sib_high,
        sib_low,
        far,
        leaf_schur,
        *skels[1:],
    )
    own_core = swapped(own, "blk", 1)
    own_chip = swapped(own, "blk", 2)

    left_high, left_low = pl.pallas_call(
        left_kernel,
        grid=(NEAR,),
        in_specs=[
            pl.BlockSpec((LEAF, RANK), lambda m: (0, 1)),
            pl.BlockSpec((1, LEAF, LEAF), lambda m: (m, 0, 0)),
            anywhere(),
        ],
        out_specs=[pl.BlockSpec((1, RANK, LEAF), lambda m: (m, 0, 0))] * 2,
        out_shape=[jax.ShapeDtypeStruct((NEAR, RANK, LEAF), b16)] * 2,
        scratch_shapes=[pltpu.VMEM((RANK, LEAF), b16)] * 2,
        compiler_params=params(),
        cost_estimate=pl.CostEstimate(flops=1, bytes_accessed=1, transcendentals=0),

        name="left_products",
    )(basis, near, own)
    base_core = swapped(after(parent_basis, left_high), "blk", 1)
    base_both = swapped(after(base_chip, left_high, prev_load, next_load), "blk", 1)
    bases = [parent_basis, base_core, base_chip, base_both]
    dma = pltpu.SemaphoreType.DMA
    loads = [
        pltpu.VMEM((2, GROUP * RANK + ROWS, RANK), f32),
        pltpu.VMEM((PAR, PAR), f32),
        pltpu.VMEM((PAR, PAR), b16),
        pltpu.VMEM((PAR, PAR), b16),
        pltpu.VMEM((2 * RANK, PAR), b16),
        pltpu.VMEM((2 * RANK, PAR), b16),
        pltpu.VMEM((PAR, PAR), f32),
    ]
    t_high, t_low, part = call(
        chip_kernel,
        "chip_sums",
        [in_smem()] + [anywhere()] * 7,
        [((RANK, PAR), b16)] * 2 + [((PAR, PAR), f32)],
        loads + [dma((2,)), dma((GROUP,)), dma((GROUP,))],
        me,
        own,
        own_core,
        *bases,
        left_high,
        spaces=[in_vmem(), in_vmem(), anywhere()],
    )
    own_both = swapped(after(own_chip, part), "blk", 1)
    prev_load = after(prev_load, part)
    next_load = after(next_load, part)
    tiles = [pltpu.VMEM((TILE, TILE), f32)] * 2
    work, edge_rows = call(
        parent_kernel,
        "parent_factor",
        [in_smem()] + [anywhere()] * 7,
        [((PRED, WIDE), f32), ((RANK, RANK), f32)],
        loads
        + [pltpu.VMEM((PAR, PAR), f32), pltpu.VMEM((PRED, WIDE), f32)]
        + tiles
        + [dma((3,)), dma((GROUP,)), dma((2,))],
        me,
        own_chip,
        own_both,
        *bases,
        part,
        spaces=[anywhere(), in_vmem()],
        limit=32 * MIB,
    )
    from_prev = gathered(prev_load, "blk", edge_rows)
    from_next = gathered(next_load, "blk", edge_rows)

    def windows(members, name, earlier):
        count = len(members)
        return call(
            functools.partial(side_kernel, blocks, members),
            name,
            [in_smem()] * 3 + [anywhere()] * (4 + 2 * count),
            [((RANK, 2 * RANK), f32)],
            [
                pltpu.VMEM((2 * count, LEAF + RANK, RANK), f32),
                pltpu.VMEM((2 * count, RANK, LEAF), b16),
                pltpu.VMEM((2 * count, RANK, LEAF), b16),
                pltpu.VMEM((2 * count, RANK, RANK), f32),
                pltpu.VMEM((RANK, count * RANK), b16),
                pltpu.VMEM((RANK, count * RANK), b16),
                pltpu.VMEM((count * RANK, RANK), b16),
                pltpu.VMEM((count * RANK, RANK), b16),
                dma((3, 2 * count)),
            ],
            me,
            near_index,
            far_index,
            left_high,
            left_low,
            far,
            *[from_prev[s] for s in members],
            *[from_next[s] for s in members],
            earlier,
            limit=24 * MIB,
        )[0]

    side = windows((0, 1, 2, 3), "side_windows", edge_rows)
    factor_rows, edge_rows = call(
        finish_kernel,
        "parent_finish",
        [in_smem(), anywhere(), in_vmem(), anywhere()],
        [((RANK, PRED), f32), ((RANK, RANK), f32)],
        [pltpu.VMEM((PRED, WIDE), f32)] + tiles + [pltpu.SemaphoreType.DMA((2,))],
        me,
        work,
        edge_rows,
        side,
        limit=16 * MIB,
    )
    sides = gathered(side, "blk", edge_rows)
    (coupling_rows,) = call(
        couple_kernel,
        "coupling",
        [in_vmem()] * 7,
        [((RANK, 3 * RANK), f32)],
        [],
        t_high,
        t_low,
        *sides,
        edge_rows,
        limit=16 * MIB,
    )
    return (leaf_out, factor_rows, coupling_rows)


def solution(mesh):
    placed = (
        P("blk", None, None),
        P("blk", None, None, None),
        P("blk", None, None, None),
        P("blk", None, None),
        P("blk", None),
        P("blk", None),
        P("blk", None),
    )
    return jax.shard_map(
        on_device,
        mesh=mesh,
        in_specs=placed,
        out_specs=(P("blk", None), P("blk", None), P("blk", None)),
        check_vma=False,
    )
```

```python
import functools

import jax
import jax.numpy as jnp
from jax import lax
from jax.experimental import pallas as pl
from jax.experimental.pallas import tpu as pltpu
from jax.sharding import PartitionSpec as P

LEAF = 512
RANK = 256
NEAR = 6
GROUP = 4
REDUN = 256
PAR = 1024
PRED = 768
FAR = 5
TILE = 128
ROWS = 8
WIDE = PRED + 2 * RANK
EARLY = 4
AHEAD = 2
MIDDLE = 30_000_000_000

MIB = 1024 * 1024
VMEM_BYTES = 64 * MIB
VMEM_EARLY = 48 * MIB

NN = (((1,), (0,)), ((), ()))
TN = (((0,), (0,)), ((), ()))


def params(limit=VMEM_BYTES):
    return pltpu.CompilerParams(vmem_limit_bytes=limit)


def in_vmem():
    return pl.BlockSpec(memory_space=pltpu.VMEM)


def in_smem():
    return pl.BlockSpec(memory_space=pltpu.SMEM)


def split(value):
    high = value.astype(jnp.bfloat16)
    low = (value - high.astype(jnp.float32)).astype(jnp.bfloat16)
    return high, low


def dot3(left, right, dims=NN):
    def one(a, b):
        return lax.dot_general(a, b, dims, preferred_element_type=jnp.float32)

    return one(left[0], right[0]) + (one(left[0], right[1]) + one(left[1], right[0]))


def lane_spread(value, lane):
    return jnp.broadcast_to(value[:, lane : lane + 1], (ROWS, TILE))


def row_spread(value, row):
    return jnp.broadcast_to(value[row : row + 1, :], (ROWS, TILE))


def small_inverse(entry):
    entry = dict(entry)
    low = {}
    inv = {}
    for j in range(ROWS):
        root = lax.rsqrt(entry[j, j])
        for i in range(j + 1, ROWS):
            low[i, j] = entry[i, j] * root
        for k in range(j + 1, ROWS):
            for i in range(k, ROWS):
                entry[i, k] = entry[i, k] - low[i, j] * low[k, j]
        inv[j, j] = root
        for t in range(j):
            total = low[j, t] * inv[t, t]
            for k in range(t + 1, j):
                total = total + low[j, k] * inv[k, t]
            inv[j, t] = -(total * root)
    return inv


def weighted(inv, j, values):
    total = inv[j, 0] * values[0]
    for t in range(1, j + 1):
        total = total + inv[j, t] * values[t]
    return total


def added(terms):
    while len(terms) > 1:
        terms = [terms[i] + terms[i + 1] for i in range(0, len(terms), 2)]
    return terms[0]


def tile_factor(square):
    count = TILE // ROWS
    row = lax.broadcasted_iota(jnp.int32, (ROWS, TILE), 0)
    col = lax.broadcasted_iota(jnp.int32, (ROWS, TILE), 1)
    left = [square[ROWS * i : ROWS * (i + 1), :] for i in range(count)]
    right = [jnp.where(row + ROWS * i == col, 1.0, 0.0).astype(jnp.float32) for i in range(count)]
    upper = []
    inverse = []
    pad1 = jnp.zeros((ROWS, TILE), jnp.float32)
    pad2 = jnp.zeros((ROWS, 2 * TILE), jnp.float32)
    cols = [lane_spread(left[0], j) for j in range(ROWS)]
    for k in range(count):
        inv = small_inverse(
            {(i, j): row_spread(cols[j], i) for j in range(ROWS) for i in range(j, ROWS)}
        )
        soon = range(k + 1, min(k + 1 + AHEAD, count))
        sides = {}
        for i in soon:
            raw = [lane_spread(left[i], ROWS * k + t) for t in range(ROWS)]
            sides[i] = [weighted(inv, j, raw) for j in range(ROWS)]
        if k + 1 < count:
            side = sides[k + 1]
            cols = [
                lane_spread(left[k + 1], ROWS * (k + 1) + j)
                - added([side[t] * row_spread(side[t], j) for t in range(ROWS)])
                for j in range(ROWS)
            ]
        u_rows = m_rows = None
        for j in range(ROWS):
            weight = inv[ROWS - 1, j]
            for i in range(ROWS - 2, j - 1, -1):
                weight = jnp.where(row == i, inv[i, j], weight)
            if j > 0:
                weight = jnp.where(row >= j, weight, 0.0)
            u_term = weight * row_spread(left[k], j)
            m_term = weight * row_spread(right[k], j)
            u_rows = u_term if u_rows is None else u_rows + u_term
            m_rows = m_term if m_rows is None else m_rows + m_term
        u_rows = jnp.where(col >= row + ROWS * k, u_rows, 0.0)
        upper.append(u_rows)
        inverse.append(m_rows)
        for i in soon:
            left[i] = left[i] - added([sides[i][j] * row_spread(u_rows, j) for j in range(ROWS)])
            right[i] = right[i] - added([sides[i][j] * row_spread(m_rows, j) for j in range(ROWS)])
        if k + 1 + AHEAD >= count:
            continue
        both = jnp.concatenate([u_rows, m_rows], axis=1)
        high = both.astype(jnp.bfloat16).astype(jnp.float32)
        low = both - high
        lhs = jnp.concatenate([high[:, :TILE], high[:, :TILE], low[:, :TILE], pad1], axis=0)
        rhs = jnp.concatenate([high, low, high, pad2], axis=0)
        update = lax.dot_general(
            lhs.astype(jnp.bfloat16),
            rhs.astype(jnp.bfloat16),
            TN,
            preferred_element_type=jnp.float32,
        )
        for i in range(k + 1 + AHEAD, count):
            rows = slice(ROWS * i, ROWS * (i + 1))
            left[i] = left[i] - update[rows, :TILE]
            right[i] = right[i] - update[rows, TILE:]
    return jnp.concatenate(upper, axis=0), jnp.concatenate(inverse, axis=0)


def leaf_kernel(diag_ref, basis_ref, after1, out_ref, schur_ref, work, u_tile, m_tile):
    basis = split(basis_ref[...])
    half = split(dot3(split(diag_ref[...]), basis))
    redundant = [part[:, :REDUN] for part in basis]
    skeleton = [part[:, REDUN:] for part in basis]
    top = dot3(redundant, half, TN)
    square = top[:, :REDUN]
    work[:, :REDUN] = 0.5 * (square + square.T)
    work[:, REDUN:] = top[:, REDUN:]
    schur_ref[...] = dot3(skeleton, [part[:, REDUN:] for part in half], TN)

    def step(k, carry):
        rows = pl.ds(pl.multiple_of(k * TILE, TILE), TILE)
        upper, inverse = tile_factor(work[rows, rows])
        u_tile[...] = upper
        m_tile[...] = inverse
        new_rows = dot3(split(m_tile[...]), split(work[rows, :]))
        work[rows, :] = new_rows
        work[rows, rows] = u_tile[...]

        @pl.when(k == 0)
        def _():
            parts = split(new_rows)
            side = [part[:, TILE:REDUN] for part in parts]
            work[TILE:, TILE:] = work[TILE:, TILE:] - dot3(side, [part[:, TILE:] for part in parts], TN)

        return carry

    lax.fori_loop(0, REDUN // TILE, step, 0)
    row = lax.broadcasted_iota(jnp.int32, (REDUN, REDUN), 0)
    col = lax.broadcasted_iota(jnp.int32, (REDUN, REDUN), 1)
    out_ref[:, :REDUN] = jnp.where(row <= col, work[:, :REDUN], 0.0).T
    coupled = work[:, REDUN:]
    out_ref[:, REDUN:] = coupled
    parts = split(coupled)
    schur_ref[...] = schur_ref[...] - dot3(parts, parts, TN)


def left_kernel(skel_ref, near_ref, after1, high_ref, low_ref, skel_high, skel_low):
    @pl.when(pl.program_id(0) == 0)
    def _():
        high, low = split(skel_ref[...].T)
        skel_high[...] = high
        skel_low[...] = low

    high, low = split(dot3((skel_high[...], skel_low[...]), split(near_ref[0])))
    high_ref[0] = high
    low_ref[0] = low


def source_of(leaf, near_ref, far_ref):
    slot = jnp.int32(0)
    for m in range(NEAR):
        slot = slot + jnp.where(near_ref[0, m] == leaf, m, 0)
    for f in range(FAR):
        slot = slot + jnp.where(far_ref[0, f] == leaf, NEAR + f, 0)
    return slot, jnp.minimum(slot, NEAR - 1), jnp.maximum(slot - NEAR, 0)


def sibling_slots(me_ref, near_ref, far_ref):
    return [source_of(jnp.bitwise_xor(me_ref[0], s), near_ref, far_ref) for s in range(1, GROUP)]


def sibling_kernel(me_ref, near_ref, far_ref, skel_ref, near_hbm, high_ref, low_ref, held, sems):
    slots = sibling_slots(me_ref, near_ref, far_ref)
    copies = [
        pltpu.make_async_copy(near_hbm.at[m], held.at[s], sems.at[s])
        for s, (_, m, _) in enumerate(slots)
    ]
    for copy in copies:
        copy.start()
    skel = split(skel_ref[...].T)
    for s in range(GROUP - 1):
        copies[s].wait()

        @pl.when(slots[s][0] < NEAR)
        def _(s=s):
            high, low = split(dot3(skel, split(held[s])))
            high_ref[s] = high
            low_ref[s] = low


def block_rows(s):
    return slice(s * RANK, (s + 1) * RANK)


def own_kernel(
    me_ref, near_ref, far_ref, high_hbm, low_hbm, far_hbm, schur_hbm, s1, s2, s3,
    out_ref, high_held, low_held, skel_held, sems, own_sem,
):
    slots = sibling_slots(me_ref, near_ref, far_ref)
    own_copy = pltpu.make_async_copy(schur_hbm, out_ref.at[block_rows(0), :], own_sem)
    near_copies = []
    far_copies = []
    for s, sibling in enumerate((s1, s2, s3)):
        near_copies.append(
            [
                pltpu.make_async_copy(high_hbm.at[s], high_held.at[s], sems.at[0, s]),
                pltpu.make_async_copy(low_hbm.at[s], low_held.at[s], sems.at[1, s]),
                pltpu.make_async_copy(sibling, skel_held.at[s], sems.at[2, s]),
            ]
        )
        far_copies.append(
            pltpu.make_async_copy(
                far_hbm.at[slots[s][2]], out_ref.at[block_rows(s + 1), :], sems.at[0, s]
            )
        )

        @pl.when(slots[s][0] < NEAR)
        def _(s=s):
            for copy in near_copies[s]:
                copy.start()

        @pl.when(slots[s][0] >= NEAR)
        def _(s=s):
            far_copies[s].start()

    own_copy.start()
    out_ref[GROUP * RANK :, :] = jnp.zeros((ROWS, RANK), jnp.float32)
    for s in range(GROUP - 1):

        @pl.when(slots[s][0] < NEAR)
        def _(s=s):
            for copy in near_copies[s]:
                copy.wait()
            out_ref[block_rows(s + 1), :] = dot3((high_held[s], low_held[s]), split(skel_held[s]))

        @pl.when(slots[s][0] >= NEAR)
        def _(s=s):
            far_copies[s].wait()

    own_copy.wait()


def side_kernel(blocks, shift, me_ref, near_ref, far_ref, high_hbm, low_hbm, far_hbm, *rest):
    count = GROUP
    zs, (after1, out_ref, z_held, high_held, low_held, far_held, h_high, h_low, s_high, s_low, sems) = (
        rest[:count],
        rest[count:],
    )
    slots = []
    z_copies = []
    near_copies = []
    far_copies = []
    for n in range(count):
        leaf = lax.rem(jnp.bitwise_xor(me_ref[0], n) + shift, blocks)
        slot, m, f = source_of(leaf, near_ref, far_ref)
        slots.append(slot)
        z_copies.append(pltpu.make_async_copy(zs[n], z_held.at[n], sems.at[0, n]))
        near_copies.append(
            [
                pltpu.make_async_copy(high_hbm.at[m], high_held.at[n], sems.at[1, n]),
                pltpu.make_async_copy(low_hbm.at[m], low_held.at[n], sems.at[2, n]),
            ]
        )
        far_copies.append(pltpu.make_async_copy(far_hbm.at[f], far_held.at[n], sems.at[1, n]))
    for n in range(count):
        z_copies[n].start()

        @pl.when(slots[n] < NEAR)
        def _(n=n):
            for copy in near_copies[n]:
                copy.start()

        @pl.when(slots[n] >= NEAR)
        def _(n=n):
            far_copies[n].start()

    for n in range(count):
        cols = block_rows(n)
        z_copies[n].wait()

        @pl.when(slots[n] < NEAR)
        def _(n=n, cols=cols):
            for copy in near_copies[n]:
                copy.wait()
            high, low = split(dot3((high_held[n], low_held[n]), split(z_held[n, :LEAF, :])))
            h_high[:, cols] = high
            h_low[:, cols] = low

        @pl.when(slots[n] >= NEAR)
        def _(n=n, cols=cols):
            far_copies[n].wait()
            high, low = split(far_held[n])
            h_high[:, cols] = high
            h_low[:, cols] = low

        high, low = split(z_held[n, LEAF:, :])
        s_high[cols, :] = high
        s_low[cols, :] = low
    out_ref[...] = dot3((h_high[...], h_low[...]), (s_high[...], s_low[...]))


def partial_sums(p_high, p_low, h_refs, first, v_high, v_low):
    for s in range(2):
        line = [h_refs[s][block_rows((first + s) ^ t), :] for t in range(GROUP)]
        line = split(jnp.concatenate(line, axis=1))
        high, low = split(dot3(line, (p_high[...], p_low[...])))
        rows = slice(s * RANK, (s + 1) * RANK)
        v_high[rows, :] = high
        v_low[rows, :] = low


def load_bases(p_hbm, p_held, p_high, p_low, sems):
    copies = []
    for s, base in enumerate(p_hbm):
        rows = block_rows(s)
        copies.append(pltpu.make_async_copy(base, p_held.at[rows, :], sems.at[s]))
        copies[s].start()

    def finish(use=None):
        for s in range(GROUP):
            rows = block_rows(s)
            copies[s].wait()
            high, low = split(p_held[rows, :])
            p_high[rows, :] = high
            p_low[rows, :] = low
            if use is not None:
                use(rows)

    return finish


def chip_kernel(
    me_ref, h0, h1, p0, p1, p2, p3, after1, t_high, t_low, part_hbm,
    h_held, p_held, p_high, p_low, v_high, v_low, part, sems, p_sems, o_sems,
):
    member = lax.rem(me_ref[0], GROUP)
    slab = pl.ds(pl.multiple_of(member * RANK, RANK), RANK)
    finish = load_bases((p0, p1, p2, p3), p_held, p_high, p_low, p_sems)
    copies = [pltpu.make_async_copy(h, h_held.at[s], sems.at[s]) for s, h in enumerate((h0, h1))]
    for copy in copies:
        copy.start()

    def own_slab(rows):
        high, low = split(p_held[rows, slab].T)
        t_high[:, rows] = high
        t_low[:, rows] = low

    finish(own_slab)
    for copy in copies:
        copy.wait()
    partial_sums(p_high, p_low, h_held, 0, v_high, v_low)
    half = slice(0, 2 * RANK)
    sent = []
    for m in range(GROUP):
        cols = block_rows(m)
        part[cols, :] = dot3((p_high[half, cols], p_low[half, cols]), (v_high[...], v_low[...]), TN)
        sent.append(pltpu.make_async_copy(part.at[cols, :], part_hbm.at[cols, :], o_sems.at[m]))
        sent[m].start()
    for copy in sent:
        copy.wait()


def eliminate(work, u_tile, m_tile, first, last, before_last=None):
    def step(k, carry):
        if before_last is not None:
            pl.when(k == last - 1)(before_last)
        rows = pl.ds(pl.multiple_of(k * TILE, TILE), TILE)
        upper, inverse = tile_factor(work[rows, rows])
        u_tile[...] = upper
        m_tile[...] = inverse
        new_rows = dot3(split(m_tile[...]), split(work[rows, :]))
        work[rows, :] = new_rows
        work[rows, rows] = u_tile[...]
        parts = split(new_rows)
        for i in range(first + 1, PRED // TILE):

            @pl.when(i > k)
            def _(i=i):
                below = slice(i * TILE, (i + 1) * TILE)
                side = [part[:, below] for part in parts]
                right = [part[:, i * TILE :] for part in parts]
                work[below, i * TILE :] = work[below, i * TILE :] - dot3(side, right, TN)

        return carry

    lax.fori_loop(first, last, step, 0)


def parent_kernel(
    me_ref, h2, h3, p0, p1, p2, p3, part_hbm, work_hbm, edge_ref,
    h_held, p_held, p_high, p_low, v_high, v_low, part, whole, work, u_tile, m_tile, sems, p_sems, o_sems,
):
    member = lax.rem(me_ref[0], GROUP)
    copies = [pltpu.make_async_copy(h, h_held.at[s], sems.at[s]) for s, h in enumerate((h2, h3))]
    for copy in copies:
        copy.start()
    finish = load_bases((p0, p1, p2, p3), p_held, p_high, p_low, p_sems)
    part_copy = pltpu.make_async_copy(part_hbm, part, sems.at[2])
    part_copy.start()
    finish()
    for copy in copies:
        copy.wait()
    partial_sums(p_high, p_low, h_held, 2, v_high, v_low)
    half = slice(2 * RANK, PAR)
    part_copy.wait()
    for m in range(GROUP):
        cols = block_rows(m)
        whole[cols, :] = part[cols, :] + dot3(
            (p_high[half, cols], p_low[half, cols]), (v_high[...], v_low[...]), TN
        )
    square = whole[:PRED, :PRED]
    work[:, :PRED] = 0.5 * (square + square.T)
    work[:, PRED:PAR] = whole[:PRED, PRED:]
    work[:, PAR:] = whole[PRED:, :PRED].T
    slab = pl.ds(pl.multiple_of(member * RANK, RANK), RANK)
    edge_ref[...] = whole[slab, PRED:]
    done = (EARLY - 1) * TILE
    held_rows = pltpu.make_async_copy(work.at[:done, :], work_hbm.at[:done, :], o_sems.at[0])
    open_rows = pltpu.make_async_copy(work.at[done:, :], work_hbm.at[done:, :], o_sems.at[1])
    eliminate(work, u_tile, m_tile, 0, EARLY, held_rows.start)
    open_rows.start()
    held_rows.wait()
    open_rows.wait()


def finish_kernel(me_ref, work_hbm, edge_in, after1, factor_ref, edge_ref, work, u_tile, m_tile, sems):
    member = lax.rem(me_ref[0], GROUP)
    done = EARLY * TILE
    open_rows = pltpu.make_async_copy(work_hbm.at[done:, :], work.at[done:, :], sems.at[0])
    held_rows = pltpu.make_async_copy(work_hbm.at[:done, :], work.at[:done, :], sems.at[1])
    open_rows.start()
    held_rows.start()
    open_rows.wait()
    eliminate(work, u_tile, m_tile, EARLY, PRED // TILE)
    held_rows.wait()
    row = lax.broadcasted_iota(jnp.int32, (PRED, RANK), 0)
    col = lax.broadcasted_iota(jnp.int32, (PRED, RANK), 1) + member * RANK
    slab = pl.ds(pl.multiple_of(member * RANK, RANK), RANK)
    factor_ref[...] = jnp.where(row <= col, work[:, slab], 0.0).T
    edge_ref[...] = edge_in[...]

    @pl.when(member == GROUP - 1)
    def _():
        product = dot3(split(work[:, PAR:]), split(work[:, PRED:PAR]), TN)
        edge_ref[...] = edge_in[...] - product


def couple_kernel(t_high, t_low, *rest):
    sides, (edge_ref, out_ref) = rest[: 2 * GROUP], rest[2 * GROUP :]
    out_ref[:, RANK : 2 * RANK] = edge_ref[...]
    for side in range(2):
        total = jnp.zeros((RANK, RANK), jnp.float32)
        for s in range(GROUP):
            cols = block_rows(s)
            total = total + dot3(
                (t_high[:, cols], t_low[:, cols]), split(sides[side * GROUP + s][...])
            )
        start = 2 * side * RANK
        out_ref[:, start : start + RANK] = total


def swapped(value, axis, mask):
    pairs = [(source, source ^ mask) for source in range(lax.axis_size(axis))]
    return lax.ppermute(value, axis, pairs)


def shifted(value, axis, steps):
    count = lax.axis_size(axis)
    pairs = [(source, (source + steps) % count) for source in range(count)]
    return lax.ppermute(value, axis, pairs)


def after(value, *earlier):
    return lax.optimization_barrier((value, *earlier))[0]


def gathered(value, axis, *earlier):
    core = swapped(value, axis, 1)
    chip = swapped(value, axis, 2)
    both = swapped(after(chip, *earlier), axis, 1)
    return [value, core, chip, both]


def call(kernel, name, ins, outs, scratch, *operands, flops=1, spaces=None, limit=VMEM_BYTES):
    return pl.pallas_call(
        kernel,
        in_specs=ins,
        out_specs=spaces or [in_vmem()] * len(outs),
        out_shape=[jax.ShapeDtypeStruct(shape, dtype) for shape, dtype in outs],
        scratch_shapes=scratch,
        compiler_params=params(limit),
        cost_estimate=pl.CostEstimate(flops=flops, bytes_accessed=1, transcendentals=0),

        name=name,
    )(*operands)


def anywhere():
    return pl.BlockSpec(memory_space=pl.ANY)


def on_device(
    diag_block, near_blocks, far_coupling, leaf_basis, parent_basis, near_index, far_index
):
    blocks = lax.axis_size("blk")
    me = lax.axis_index("blk").astype(jnp.int32).reshape(1)
    basis = leaf_basis[0]
    skeleton = basis[:, REDUN:]
    near = near_blocks[0]
    far = far_coupling[0]
    f32, b16 = jnp.float32, jnp.bfloat16

    load = jnp.concatenate([skeleton, parent_basis[:, PRED:]], axis=0)
    prev_load = shifted(load, "blk", GROUP)
    next_load = shifted(load, "blk", -GROUP)

    base_chip = swapped(parent_basis, "blk", 2)

    sib_high, sib_low = call(
        sibling_kernel,
        "sibling_products",
        [in_smem()] * 3 + [in_vmem(), anywhere()],
        [((GROUP - 1, RANK, LEAF), b16)] * 2,
        [pltpu.VMEM((GROUP - 1, LEAF, LEAF), f32), pltpu.SemaphoreType.DMA((GROUP - 1,))],
        me,
        near_index,
        far_index,
        skeleton,
        near,
        limit=VMEM_EARLY,
    )
    leaf_out, leaf_schur = call(
        leaf_kernel,
        "leaf_factor",
        [in_vmem()] * 2 + [anywhere()],
        [((REDUN, LEAF), f32), ((RANK, RANK), f32)],
        [pltpu.VMEM((REDUN, LEAF), f32), pltpu.VMEM((TILE, TILE), f32), pltpu.VMEM((TILE, TILE), f32)],
        diag_block[0],
        basis,
        sib_high,
        flops=MIDDLE,
        limit=VMEM_EARLY,
    )
    skel_chip = swapped(skeleton, "blk", 2)
    skel_core = swapped(skeleton, "blk", 1)
    skels = [skeleton, skel_core, skel_chip, swapped(skel_chip, "blk", 1)]
    (own,) = call(
        own_kernel,
        "own_window",
        [in_smem()] * 3 + [anywhere()] * 7,
        [((GROUP * RANK + ROWS, RANK), f32)],
        [pltpu.VMEM((GROUP - 1, RANK, LEAF), b16)] * 2
        + [
            pltpu.VMEM((GROUP - 1, LEAF, RANK), f32),
            pltpu.SemaphoreType.DMA((3, GROUP - 1)),
            pltpu.SemaphoreType.DMA,
        ],
        me,
        near_index,
        far_index,
        sib_high,
        sib_low,
        far,
        leaf_schur,
        *skels[1:],
    )
    own_core = swapped(own, "blk", 1)
    own_chip = swapped(own, "blk", 2)

    left_high, left_low = pl.pallas_call(
        left_kernel,
        grid=(NEAR,),
        in_specs=[
            pl.BlockSpec((LEAF, RANK), lambda m: (0, 1)),
            pl.BlockSpec((1, LEAF, LEAF), lambda m: (m, 0, 0)),
            anywhere(),
        ],
        out_specs=[pl.BlockSpec((1, RANK, LEAF), lambda m: (m, 0, 0))] * 2,
        out_shape=[jax.ShapeDtypeStruct((NEAR, RANK, LEAF), b16)] * 2,
        scratch_shapes=[pltpu.VMEM((RANK, LEAF), b16)] * 2,
        compiler_params=params(),
        cost_estimate=pl.CostEstimate(flops=1, bytes_accessed=1, transcendentals=0),

        name="left_products",
    )(basis, near, own)
    base_core = swapped(after(parent_basis, left_high), "blk", 1)
    base_both = swapped(after(base_chip, left_high, prev_load, next_load), "blk", 1)
    bases = [parent_basis, base_core, base_chip, base_both]
    dma = pltpu.SemaphoreType.DMA
    loads = [
        pltpu.VMEM((2, GROUP * RANK + ROWS, RANK), f32),
        pltpu.VMEM((PAR, PAR), f32),
        pltpu.VMEM((PAR, PAR), b16),
        pltpu.VMEM((PAR, PAR), b16),
        pltpu.VMEM((2 * RANK, PAR), b16),
        pltpu.VMEM((2 * RANK, PAR), b16),
        pltpu.VMEM((PAR, PAR), f32),
    ]
    t_high, t_low, part = call(
        chip_kernel,
        "chip_sums",
        [in_smem()] + [anywhere()] * 7,
        [((RANK, PAR), b16)] * 2 + [((PAR, PAR), f32)],
        loads + [dma((2,)), dma((GROUP,)), dma((GROUP,))],
        me,
        own,
        own_core,
        *bases,
        left_high,
        spaces=[in_vmem(), in_vmem(), anywhere()],
    )
    own_both = swapped(after(own_chip, part), "blk", 1)
    prev_load = after(prev_load, part)
    next_load = after(next_load, part)
    tiles = [pltpu.VMEM((TILE, TILE), f32)] * 2
    work, edge_rows = call(
        parent_kernel,
        "parent_factor",
        [in_smem()] + [anywhere()] * 7,
        [((PRED, WIDE), f32), ((RANK, RANK), f32)],
        loads
        + [pltpu.VMEM((PAR, PAR), f32), pltpu.VMEM((PRED, WIDE), f32)]
        + tiles
        + [dma((3,)), dma((GROUP,)), dma((2,))],
        me,
        own_chip,
        own_both,
        *bases,
        part,
        spaces=[anywhere(), in_vmem()],
        limit=32 * MIB,
    )
    from_prev = gathered(prev_load, "blk", edge_rows)
    from_next = gathered(next_load, "blk", edge_rows)

    def windows(shift, name, loads, earlier):
        return call(
            functools.partial(side_kernel, blocks, shift),
            name,
            [in_smem()] * 3 + [anywhere()] * (GROUP + 4),
            [((RANK, RANK), f32)],
            [
                pltpu.VMEM((GROUP, LEAF + RANK, RANK), f32),
                pltpu.VMEM((GROUP, RANK, LEAF), b16),
                pltpu.VMEM((GROUP, RANK, LEAF), b16),
                pltpu.VMEM((GROUP, RANK, RANK), f32),
                pltpu.VMEM((RANK, PAR), b16),
                pltpu.VMEM((RANK, PAR), b16),
                pltpu.VMEM((PAR, RANK), b16),
                pltpu.VMEM((PAR, RANK), b16),
                dma((3, GROUP)),
            ],
            me,
            near_index,
            far_index,
            left_high,
            left_low,
            far,
            *loads,
            earlier,
            limit=24 * MIB,
        )[0]

    prev_side = windows(blocks - GROUP, "prev_windows", from_prev, edge_rows)
    next_side = windows(GROUP, "next_windows", from_next, prev_side)
    factor_rows, edge_rows = call(
        finish_kernel,
        "parent_finish",
        [in_smem(), anywhere(), in_vmem(), anywhere()],
        [((RANK, PRED), f32), ((RANK, RANK), f32)],
        [pltpu.VMEM((PRED, WIDE), f32)] + tiles + [pltpu.SemaphoreType.DMA((2,))],
        me,
        work,
        edge_rows,
        next_side,
        limit=16 * MIB,
    )
    prev_sides = gathered(prev_side, "blk", edge_rows)
    next_sides = gathered(next_side, "blk", edge_rows)
    (coupling_rows,) = call(
        couple_kernel,
        "coupling",
        [in_vmem()] * 11,
        [((RANK, 3 * RANK), f32)],
        [],
        t_high,
        t_low,
        *prev_sides,
        *next_sides,
        edge_rows,
        limit=16 * MIB,
    )
    return (leaf_out, factor_rows, coupling_rows)


def solution(mesh):
    placed = (
        P("blk", None, None),
        P("blk", None, None, None),
        P("blk", None, None, None),
        P("blk", None, None),
        P("blk", None),
        P("blk", None),
        P("blk", None),
    )
    return jax.shard_map(
        on_device,
        mesh=mesh,
        in_specs=placed,
        out_specs=(P("blk", None), P("blk", None), P("blk", None)),
        check_vma=False,
    )
```
